128 devices in a mesh: seq: 16 (over x_hi, y, core), chan: 8 (over z, x_lo).
Axes of the slice: x: 4 (x_hi: 2, x_lo: 2; x = x_hi * 2 + x_lo), y: 4, z: 4, core: 2. Of those that a mesh axis runs over, the one named last changes fastest.
Arguments:
- residual_in: bfloat16 [4096, 4096], P('seq', 'chan')
- mr_query: bfloat16 [4096, 4096], P('seq', 'chan'), may hold values from -6 to 6
- mr_key: bfloat16 [4096, 4096], P('seq', 'chan'), may hold values from -6 to 6
- mr_value: bfloat16 [4096, 4096], P('seq', 'chan'), may hold values from -6 to 6
- mr_short: bfloat16 [3, 3, 4096], P(None, None, 'chan'), may hold values from -3.5 to 3.5
- mr_filter: bfloat16 [128, 4096], P(None, 'chan'), may hold values from -0.5 to 0.5
- mix_weight: bfloat16 [4096, 4096], P('chan'), may hold values from -0.125 to 0.125
- norm_gain: bfloat16 [4096], P('chan'), may hold values from 0.099609375 to 1.8984375
- li_weight: bfloat16 [3, 4096, 4096], P(None, None, 'chan'), may hold values from -0.09375 to 0.09375
- li_short: bfloat16 [3, 3, 4096], P(None, None, 'chan'), may hold values from -3.5 to 3.5
- li_rate: float32 [4096, 16], P('chan'), as said below
- li_residue: float32 [4096, 16], P('chan')
- decode_slot: int32 [128], P('chan'), may hold values from 0 to 127, as said below
Outputs:
- li_out: bfloat16 [4096, 4096], P('seq', 'chan')
- residual_out: bfloat16 [4096, 4096], P('seq', 'chan')
- decode_state: float32 [128, 512], P(('seq', 'chan'))
The draws below stay inside these ranges and needn't reach their ends.
Inputs may be any that keep to these rules, and one draw needn't show every extreme that they name: `decode_slot`: the 128 slots are distinct; the slot q of block b satisfies (q) % 8 == b // 16. `li_rate`: positive decay rates.
All inputs are finite; a program needn't handle non-finite values.
Results may differ from the reference program's by a relative error of at most 0.035.
Values may be sent and summed in bfloat16 or wider, within the bound.
A program may use at most 320 MiB of HBM per device.

```python
import math
import jax
import jax.numpy as jnp
from jax import lax

D = 4096
MODES = 16
MR_TAPS = 128
SHORT = 3
CB = 32
BLK = 128
SEQ_LEN = 4096
GROUPS = 8
BLOCKS = 128
BPG = 16
OWN = 1


def mode_rates(key, slow_share):
    key_pick, key_slow, key_fast = jax.random.split(key, 3)
    slowness = jax.random.uniform(key_pick, (D, MODES), jnp.float32)
    slow_rate = jnp.exp(jax.random.uniform(key_slow, (D, MODES), jnp.float32, math.log(0.2 / SEQ_LEN), math.log(2.0 / SEQ_LEN)))
    fast_rate = jnp.exp(jax.random.uniform(key_fast, (D, MODES), jnp.float32, math.log(1.0 / 50.0), math.log(1.0 / 30.0)))
    return jnp.where(slowness < slow_share, slow_rate, fast_rate)


def draw_li_rate(key, part):
    slow_share = 0.5
    return mode_rates(key, slow_share)


def draw_li_residue(key, part):
    slow_share = 0.5
    mode_rate = mode_rates(key, slow_share)
    key = jax.random.fold_in(key, 5)
    factor = 0.35 * jax.random.normal(key, (D, MODES), jnp.float32)
    return factor * jnp.sqrt(-jnp.expm1(-2.0 * mode_rate))


def draw_residual_in(key, part):
    key = jax.random.fold_in(key, 3)
    key_base, key_column, key_row = jax.random.split(key, 3)
    column = 0.1 * jnp.exp(math.log(10.0) * jnp.arange(D, dtype=jnp.float32) / D + jax.random.uniform(key_column, (D,), jnp.float32, 0.0, math.log(2.0)))
    row_scale = jnp.exp(jax.random.uniform(key_row, (SEQ_LEN, 1), jnp.float32, math.log(0.3), math.log(3.0)))
    base = jax.random.normal(key_base, (SEQ_LEN, D), jnp.float32)
    return (base * column[None, :] * row_scale).astype(jnp.bfloat16)


def group_order(group_key):
    return jax.random.permutation(group_key, BPG)


def draw_decode_slot(key, part):
    key = jax.random.fold_in(key, 11)
    group_keys = jax.random.split(key, GROUPS)
    orders = jax.vmap(group_order)(group_keys)
    group_column = jnp.arange(GROUPS, dtype=jnp.int32)[:, None]
    slots = (orders // OWN * GROUPS + group_column) * OWN + orders % OWN
    return slots.reshape(BLOCKS).astype(jnp.int32)


def raised(entries, own_key, source, target, parts, factor):
    owner, partner = [(jnp.arange(entries.shape[axis_at]) // (entries.shape[axis_at] // parts)).reshape([-1 if axis == axis_at else 1 for axis in range(entries.ndim)]) for axis_at in (source, target)]
    chosen = jax.random.permutation(own_key, parts)[partner]
    strong = (owner == chosen) | (owner == (partner + parts // 2) % parts)
    return jnp.where(strong, factor * entries, entries)


def level_of(rng, extent, cuts, low, largest):
    def one(dim, blocks):
        heights = jax.random.uniform(jax.random.fold_in(jax.random.fold_in(rng, 6), dim), (blocks,), jnp.float32, low / len(cuts), largest / len(cuts))
        return jnp.repeat(jnp.exp(heights), extent[dim] // blocks).reshape((-1,) + (1,) * (len(extent) - dim - 1))

    loudness = one(*cuts[0])
    for cut in cuts[1:]:
        loudness = loudness * one(*cut)
    return loudness


def scatter_about(stream_key, shape, deviation, most, pieces=(), kind=jnp.bfloat16):
    entries = deviation * jax.random.normal(stream_key, shape, jnp.float32)
    if pieces:
        entries = entries * level_of(stream_key, shape, pieces, -0.22, 0.18)
    return jnp.clip(entries, -most, most).astype(kind)


def noise_with(own_key, extent, spread, most, cuts, heavy, held_as=jnp.bfloat16):
    values = spread * jax.random.normal(own_key, extent, jnp.float32)
    if cuts:
        values = values * level_of(own_key, extent, cuts, -0.22, 0.18)
    return jnp.clip(raised(values, jax.random.fold_in(own_key, 3), *heavy), -most, most).astype(held_as)


def setup_inputs(seed: int = 0) -> dict:
    key_list = jax.random.split(jax.random.key(seed), 14)
    residual_in = draw_residual_in(jax.random.fold_in(key_list[13], 71), 0)
    mr_query = scatter_about(key_list[1], (SEQ_LEN, D), 1.0, 6.0, ((0, 16), (1, 8)))
    mr_key = scatter_about(key_list[2], (SEQ_LEN, D), 1.0, 6.0, ((0, 16), (1, 8)))
    mr_value = scatter_about(key_list[3], (SEQ_LEN, D), 1.0, 6.0, ((0, 16), (1, 8)))
    mr_short = scatter_about(key_list[4], (3, SHORT, D), SHORT ** -0.5, 3.5, ((2, 8),))
    mr_filter = scatter_about(key_list[5], (MR_TAPS, D), MR_TAPS ** -0.5, 0.5, ((1, 8),))
    mix_weight = noise_with(key_list[6], (D, D), D ** -0.5, 0.125, ((0, 8),), (0, 1, 8, 2.0))
    norm_gain = jnp.clip(1.0 + 0.18 * jax.random.normal(key_list[7], (D,), jnp.float32), 0.099609375, 1.8984375).astype(jnp.bfloat16)
    li_weight = scatter_about(key_list[8], (3, D, D), D ** -0.5, 0.09375, ((2, 8),))
    li_short = scatter_about(key_list[9], (3, SHORT, D), SHORT ** -0.5, 3.5, ((2, 8),))
    li_rate = draw_li_rate(jax.random.fold_in(key_list[13], 71), 0)
    li_residue = draw_li_residue(jax.random.fold_in(key_list[13], 71), 0)
    decode_slot = draw_decode_slot(jax.random.fold_in(key_list[13], 71), 0)
    return dict(residual_in=residual_in, mr_query=mr_query, mr_key=mr_key, mr_value=mr_value, mr_short=mr_short, mr_filter=mr_filter, mix_weight=mix_weight, norm_gain=norm_gain, li_weight=li_weight, li_short=li_short, li_rate=li_rate, li_residue=li_residue, decode_slot=decode_slot)


EPSILON = 1e-06
HIGHEST_PRECISION = lax.Precision.HIGHEST

def short_filter(extended, taps_weight, short_lead):
    out_rows = extended.shape[0] - short_lead
    running = jnp.zeros((out_rows, extended.shape[1]), jnp.float32)
    for offset in range(taps_weight.shape[0]):
        window = extended[short_lead - offset:short_lead - offset + out_rows]
        running = running + taps_weight[offset].astype(jnp.float32)[None, :] * window.astype(jnp.float32)
    return running

def tap_matrix(filter_taps, block_size):
    tap_count = filter_taps.shape[0]
    lag_grid = jnp.arange(block_size)[:, None] + block_size - jnp.arange(2 * block_size)[None, :]
    inside = (lag_grid >= 0) & (lag_grid < tap_count)
    picked = jnp.take(filter_taps, jnp.clip(lag_grid, 0, tap_count - 1), axis=0)
    return jnp.where(inside[:, :, None], picked, jnp.zeros_like(picked))

def tap_conv(extended, filter_taps, block_size):
    out_rows = extended.shape[0] - block_size
    block_count = out_rows // block_size
    earlier = extended[:out_rows].reshape(block_count, block_size, -1)
    current = extended[block_size:].reshape(block_count, block_size, -1)
    joined = jnp.concatenate([earlier, current], axis=1)
    matrix = tap_matrix(filter_taps, block_size)
    result = jnp.einsum('tsc,bsc->btc', matrix.astype(jnp.float32), joined.astype(jnp.float32), precision=HIGHEST_PRECISION)
    return result.reshape(out_rows, -1)

def modal_tables(rate_part, residue_part, block_size):
    offsets = jnp.arange(block_size, dtype=jnp.float32)
    kernel = lax.optimization_barrier(jnp.sum(residue_part[None] * jnp.exp(-rate_part[None] * offsets[:, None, None]), axis=2))
    lag_grid = jnp.arange(block_size)[:, None] - jnp.arange(block_size)[None, :]
    picked = jnp.take(kernel, jnp.maximum(lag_grid, 0), axis=0)
    lower_band = jnp.where((lag_grid >= 0)[:, :, None], picked, jnp.zeros_like(picked))
    end_weights = jnp.exp(-rate_part[None] * (block_size - 1.0 - offsets)[:, None, None])
    start_weights = residue_part[None] * jnp.exp(-rate_part[None] * (offsets + 1.0)[:, None, None])
    step_decay = jnp.exp(-rate_part * block_size)
    return (lower_band, end_weights, start_weights, step_decay)

def modal_local(input_blocks, lower_band, end_weights):
    within = jnp.einsum('tsc,bsc->btc', lower_band, input_blocks, precision=HIGHEST_PRECISION)
    block_states = jnp.einsum('tcm,btc->bcm', end_weights, input_blocks, precision=HIGHEST_PRECISION)
    return (within, block_states)

def modal_sweep(block_states, start_state, step_decay):

    def advance(carried, block_state):
        return (step_decay * carried + block_state, carried)
    leaving, entering = lax.scan(advance, start_state, block_states)
    return (leaving, entering)

def mr_group(running, inputs):
    query_part, key_part, value_part, short_taps, filter_taps, mix_rows = inputs
    short_lead = SHORT - 1
    chan_width = query_part.shape[1]
    padding = jnp.zeros((short_lead, chan_width), jnp.bfloat16)
    query_short = short_filter(jnp.concatenate([padding, query_part]), short_taps[0], short_lead)
    key_short = short_filter(jnp.concatenate([padding, key_part]), short_taps[1], short_lead)
    value_short = short_filter(jnp.concatenate([padding, value_part]), short_taps[2], short_lead)
    mr_input = (key_short * value_short).astype(jnp.bfloat16)
    extended = jnp.concatenate([jnp.zeros((BLK, chan_width), jnp.bfloat16), mr_input])
    mr_conv = tap_conv(extended, filter_taps, BLK)
    mr_gated = (query_short * mr_conv).astype(jnp.bfloat16)
    partial_value = jnp.dot(mr_gated, mix_rows, preferred_element_type=jnp.float32).astype(jnp.bfloat16)
    partial_value = lax.optimization_barrier(partial_value)
    return (running + partial_value.astype(jnp.float32), None)

def li_group(normed_wide, weight_part, short_taps, rate_part, residue_part):
    projected = jnp.einsum('td,idc->itc', normed_wide, weight_part.astype(jnp.float32), precision=HIGHEST_PRECISION).astype(jnp.bfloat16)
    short_lead = SHORT - 1
    chan_width = projected.shape[2]
    padding = jnp.zeros((3, short_lead, chan_width), jnp.bfloat16)
    extended = jnp.concatenate([padding, projected], axis=1)
    query_short = short_filter(extended[0], short_taps[0], short_lead)
    key_short = short_filter(extended[1], short_taps[1], short_lead)
    value_short = short_filter(extended[2], short_taps[2], short_lead)
    li_input = (key_short * value_short).astype(jnp.bfloat16)
    block_count = SEQ_LEN // BLK
    input_blocks = li_input.astype(jnp.float32).reshape(block_count, BLK, chan_width)
    lower_band, end_weights, start_weights, step_decay = modal_tables(rate_part, residue_part, BLK)
    within, block_states = modal_local(input_blocks, lower_band, end_weights)
    leaving, entering = modal_sweep(block_states, jnp.zeros((chan_width, MODES), jnp.float32), step_decay)
    across = jnp.einsum('tcm,bcm->btc', start_weights, entering, precision=HIGHEST_PRECISION)
    li_conv = (within + across).reshape(SEQ_LEN, chan_width)
    li_out = (query_short * li_conv).astype(jnp.bfloat16)
    return (li_out, residue_part * leaving)

def reference(residual_in, mr_query, mr_key, mr_value, mr_short, mr_filter, mix_weight, norm_gain, li_weight, li_short, li_rate, li_residue, decode_slot):
    chan_width = D // GROUPS

    def by_group(array):
        return array.reshape(SEQ_LEN, GROUPS, chan_width).transpose(1, 0, 2)
    mr_shorts = mr_short.reshape(3, SHORT, GROUPS, chan_width).transpose(2, 0, 1, 3)
    mr_filters = mr_filter.reshape(MR_TAPS, GROUPS, chan_width).transpose(1, 0, 2)
    mix_groups = mix_weight.reshape(GROUPS, chan_width, D)
    mixed, _ = lax.scan(mr_group, jnp.zeros((SEQ_LEN, D), jnp.float32), (by_group(mr_query), by_group(mr_key), by_group(mr_value), mr_shorts, mr_filters, mix_groups))
    residual_sum = residual_in.astype(jnp.float32) + mixed
    residual_out = residual_sum.astype(jnp.bfloat16)
    inverse = lax.rsqrt(lax.optimization_barrier(jnp.mean(residual_sum * residual_sum, axis=1, keepdims=True)) + EPSILON)
    normed = (residual_sum * inverse * norm_gain.astype(jnp.float32)[None, :]).astype(jnp.bfloat16)
    normed_wide = normed.astype(jnp.float32)
    li_weights = li_weight.reshape(3, D, GROUPS, chan_width).transpose(2, 0, 1, 3)
    li_shorts = li_short.reshape(3, SHORT, GROUPS, chan_width).transpose(2, 0, 1, 3)
    rate_groups = li_rate.reshape(GROUPS, chan_width, MODES)
    residue_groups = li_residue.reshape(GROUPS, chan_width, MODES)

    def run_group(inputs):
        return li_group(normed_wide, inputs[0], inputs[1], inputs[2], inputs[3])
    outputs, finals = lax.map(run_group, (li_weights, li_shorts, rate_groups, residue_groups))
    li_out = outputs.transpose(1, 0, 2).reshape(SEQ_LEN, D)
    blocks = finals.reshape(BLOCKS, CB * MODES)
    decode_state = jnp.zeros_like(blocks).at[decode_slot].set(blocks)
    return (li_out, residual_out, decode_state)
```

```python
import functools

import jax
import jax.numpy as jnp
import ml_dtypes
import numpy as np
from jax import lax
from jax.experimental import pallas as pl
from jax.experimental.pallas import tpu as pltpu
from jax.sharding import PartitionSpec as P

MESH = pl.DeviceIdType.MESH
F32 = jnp.float32
BF16 = jnp.bfloat16

D = 4096
MODES = 16
CB = 32
EPSILON = 1e-06
BIG = 1e30

R = 256
W = 512
H = 16
N = 8

LATE = ((128, 48, (0, 1, 2)), (176, 48, (1, 2, 0)), (224, 32, (2, 0, 1)))
EARLY = ((0, 48, (0, 1, 2)), (48, 32, (1, 2, 0)), (80, 48, (2, 0, 1)))
PIECES = LATE + EARLY


def fourier(period, rows_in, out_from, rows_out):
    half = period // 2
    k = np.arange(half)[:, None]
    t = np.arange(rows_in)[None, :]
    angle = 2.0 * np.pi * ((k * t) % period) / period
    real, imag = np.cos(angle), -np.sin(angle)
    imag[0] = np.where(np.arange(rows_in) % 2 == 0, 1.0, -1.0)
    forward = np.concatenate([real, imag], axis=0)
    t = (out_from + np.arange(rows_out))[:, None]
    k = np.arange(half)[None, :]
    angle = 2.0 * np.pi * ((k * t) % period) / period
    real, imag = 2.0 * np.cos(angle), -2.0 * np.sin(angle)
    real[:, 0] = 1.0
    imag[:, 0] = np.where((out_from + np.arange(rows_out)) % 2 == 0, 1.0, -1.0)
    inverse = np.concatenate([real, imag], axis=1) / period
    return forward, inverse


def bits(slot):
    return (slot >> 2) & 1, (slot >> 1) & 1, slot & 1


def picked(**fixed):
    index = [slice(None)] * 3
    for name, value in fixed.items():
        index[2 - int(name[1])] = value
    return tuple(index)


def flipped(chan, slot):
    b2, b1, b0 = bits(slot)
    z, x = chan // 2, chan % 2
    if b0:
        x = 1 - x
    if b1:
        z = z + 1 - 2 * (z % 2)
    if b2:
        z = 3 - z
    return 2 * z + x


def kernel(
    n_seq,
    res_in, q_in, k_in, v_in, mix_in, liw_in,
    mr_short, mr_filter, gain, li_short, rate, residue, slots,
    f256, g256, f512, g512,
    li_out, res_out, dec_out,
    qkv, mu, qs, ht, gated, mw, part, rb1, rb2, rb3, res_v, hb, sqc, sqs, sqr,
    lw, lp, ql, ub, table, kern, lt, urev, conv, st, sb, sr, lo_v, ro_v,
    load_sem, halo_s, halo_r, rs_s, rs_r, ag_s, ag_r, sq_s, sq_r, st_s, st_r, out_sem,
):
    seq, chan = lax.axis_index("seq"), lax.axis_index("chan")
    first = seq == 0
    pending = []

    loads = []

    def load(src, dst):
        copy = pltpu.make_async_copy(src, dst, load_sem.at[len(loads)])
        copy.start()
        loads.append(copy)
        return copy

    in_loads = [load(ref, qkv.at[i, pl.ds(H, R), :]) for i, ref in enumerate((q_in, k_in, v_in))]
    mix_loads = [
        load(mix_in.at[:, pl.ds(pl.multiple_of(flipped(chan, s) * W, W), W)], mw.at[s]) for s in range(N)
    ]
    res_load = load(res_in, res_v)
    li_loads = [
        load(liw_in.at[:, pl.ds(pl.multiple_of(flipped(chan, s) * W, W), W), :], lw.at[:, pl.ds(s * W, W), :])
        for s in range(N)
    ]

    barrier = pltpu.get_barrier_semaphore()
    seq_peers = [lax.rem(seq + k, n_seq) for k in range(1, n_seq)]
    chan_peers = [lax.rem(chan + k, N) for k in range(1, N)]
    for peer in seq_peers:
        pl.semaphore_signal(barrier, inc=1, device_id=(peer, chan), device_id_type=MESH)
    for peer in chan_peers:
        pl.semaphore_signal(barrier, inc=1, device_id=(seq, peer), device_id_type=MESH)
    pl.semaphore_wait(barrier, n_seq - 1 + N - 1)

    def send(src, dst, send_sem, recv_sem, to):
        copy = pltpu.make_async_remote_copy(
            src_ref=src, dst_ref=dst, send_sem=send_sem, recv_sem=recv_sem,
            device_id=to, device_id_type=MESH,
        )
        copy.start()
        pending.append(copy)
        return copy

    after = (lax.rem(seq + 1, n_seq), chan)
    halos = [
        send(ref.at[pl.ds(R - H, H), :], qkv.at[i, pl.ds(0, H), :], halo_s.at[i], halo_r.at[i], after)
        for i, ref in enumerate((q_in, k_in, v_in))
    ]

    spectrum = jnp.dot(f256[:, :128], mr_filter[...], preferred_element_type=F32)
    row = lax.broadcasted_iota(jnp.int32, (128, W), 0)
    ht[0] = spectrum[:128]
    ht[1] = jnp.where(row == 0, 0.0, spectrum[128:])
    ht[2] = jnp.where(row == 0, spectrum[128:], spectrum[:128])

    def short(ext, taps, rows):
        once = pltpu.roll(ext, 1, 0)
        twice = pltpu.roll(ext, 2, 0)
        top = ext.shape[0] - rows
        return taps[0:1] * ext[top:] + taps[1:2] * once[top:] + taps[2:3] * twice[top:]

    for copy in in_loads:
        copy.wait()
    for copy in halos:
        copy.wait_recv()
    mr_taps = [mr_short[i].astype(F32) for i in range(3)]
    ext_row = lax.broadcasted_iota(jnp.int32, (H + R, 128), 0)
    outside = jnp.logical_and(first, ext_row < H)
    for c in range(W // 128):
        lanes = slice(c * 128, (c + 1) * 128)
        three = []
        for i in range(3):
            ext = jnp.where(outside, 0.0, qkv[i, :, lanes].astype(F32))
            three.append(short(ext, mr_taps[i][:, lanes], R))
        qs[:, lanes] = three[0]
        mu[128:, lanes] = (three[1] * three[2]).astype(BF16)
    rim = send(mu.at[pl.ds(R, 128), :], mu.at[pl.ds(0, 128), :], halo_s.at[3], halo_r.at[3], after)

    def mr_rows(r0):
        x = jnp.dot(f256[...], mu[r0 : r0 + 256, :], preferred_element_type=F32)
        xr, xi = x[:128], x[128:]
        y = jnp.concatenate(
            [
                (xr * ht[0] - xi * ht[1]).astype(BF16),
                (xr * ht[1] + xi * ht[2]).astype(BF16),
            ],
            axis=0,
        )
        out = jnp.dot(g256[...], y, preferred_element_type=F32)
        gated[r0 : r0 + 128, :] = (qs[r0 : r0 + 128, :] * out).astype(BF16)
        for s in range(N):
            part[bits(s) + (slice(r0, r0 + 128), slice(None))] = jnp.dot(
                gated[r0 : r0 + 128, :], mw[s], preferred_element_type=F32
            ).astype(BF16)

    def rs_view(ref, g, *fixed):
        r0, n, order = PIECES[g]
        index = picked(**{f"b{order[i]}": v for i, v in enumerate(fixed)})
        return index + (pl.ds(r0, n), slice(None))

    def rs_send(g, step):
        r0, n, order = PIECES[g]
        fixed = (0,) * step + (1,)
        src = part.at[rs_view(part, g, *fixed)]
        rows = pl.ds(r0, n)
        dst = (rb1.at[:, :, rows, :], rb2.at[:, rows, :], rb3.at[rows, :])[step]
        to = (seq, flipped(chan, 1 << order[step]))
        return send(src, dst, rs_s.at[g, step], rs_r.at[g, step], to)

    def rs_add(g, step):
        r0, n, order = PIECES[g]
        rows = slice(r0, r0 + n)
        fixed = (0,) * (step + 1)
        index = rs_view(part, g, *fixed)[:3] + (rows, slice(None))
        got = (rb1[:, :, rows, :], rb2[:, rows, :])[step]
        part[index] = (part[index].astype(F32) + got.astype(F32)).astype(BF16)

    def rs_end(g):
        r0, n, order = PIECES[g]
        rows = slice(r0, r0 + n)
        total = res_v[rows, :].astype(F32) + (
            part[0, 0, 0, rows, :].astype(F32) + rb3[rows, :].astype(F32)
        )
        ro_v[rows, :] = total.astype(BF16)
        sqc[rows, :] = jnp.broadcast_to(jnp.sum(total * total, axis=1, keepdims=True), (n, 128))
        scaled = jnp.clip(total * gain[...].astype(F32), -BIG, BIG)
        hb[0, 0, 0, rows, :] = scaled.astype(BF16)

    def ag_send(g, step):
        r0, n, order = PIECES[g]
        dims = order[::-1]
        later = {f"b{d}": 0 for d in dims[step + 1 :]}
        rows = (pl.ds(r0, n), slice(None))
        src = hb.at[picked(**later, **{f"b{dims[step]}": 0}) + rows]
        dst = hb.at[picked(**later, **{f"b{dims[step]}": 1}) + rows]
        to = (seq, flipped(chan, 1 << dims[step]))
        return send(src, dst, ag_s.at[g, step], ag_r.at[g, step], to)

    def sq_send(b, r0):
        sqs[b] = sqc[r0 : r0 + 128, :].T[:8]
        return [
            send(sqs.at[b], sqr.at[b, k], sq_s.at[b, k], sq_r.at[b, k], (seq, chan_peers[k]))
            for k in range(N - 1)
        ]

    def project(b, r0, squares):
        for copy in squares:
            copy.wait_recv()
        total = sqs[b]
        for k in range(N - 1):
            total = total + sqr[b, k]
        inverse = lax.rsqrt(total / D + EPSILON)
        inverse = jnp.broadcast_to(inverse[0:1], (128, 128)).T
        wide = jnp.concatenate([inverse] * (W // 128), axis=1)
        rows = slice(r0, r0 + 128)
        lhs = jnp.concatenate([hb[bits(s) + (rows, slice(None))] for s in range(N)], axis=1)

        def one(i, carry):
            out = jnp.dot(lhs, lw[i], preferred_element_type=F32) * wide
            lp[i, H + r0 : H + r0 + 128, :] = out.astype(BF16)
            return carry

        lax.fori_loop(0, 3, one, 0)

    late, early = range(3), range(3, 6)

    for copy in mix_loads:
        copy.wait()
    mr_rows(128)
    rs = {(g, 0): rs_send(g, 0) for g in late}
    rim.wait_recv()
    mu[:128, :] = jnp.where(first, jnp.zeros((128, W), BF16), mu[:128, :])
    mr_rows(0)
    rs.update({(g, 0): rs_send(g, 0) for g in early})

    kern[...] = jnp.zeros((R, W), F32)
    time = lax.broadcasted_iota(jnp.int32, (R, W), 0).astype(F32)

    def mode(m, carry):
        powers = jnp.exp(-rate[pl.ds(m, 1), :] * time)
        table[m] = powers
        kern[...] += residue[pl.ds(m, 1), :] * powers
        return carry

    lax.fori_loop(0, MODES // 2, mode, 0)

    for group in (late, early):
        for g in group:
            rs[g, 0].wait_recv()
            rs_add(g, 0)
            rs[g, 1] = rs_send(g, 1)

    lax.fori_loop(MODES // 2, MODES, mode, 0)
    spectrum = jnp.dot(f512[:512, :], kern[...].astype(BF16), preferred_element_type=F32)
    row = lax.broadcasted_iota(jnp.int32, (256, W), 0)
    lt[0] = spectrum[:256]
    lt[1] = jnp.where(row == 0, 0.0, spectrum[256:])
    lt[2] = jnp.where(row == 0, spectrum[256:], spectrum[:256])

    for group in (late, early):
        for g in group:
            rs[g, 1].wait_recv()
            rs_add(g, 1)
            rs[g, 2] = rs_send(g, 2)
    res_load.wait()
    ag = {}
    squares = []
    for b, group in enumerate((late, early)):
        for g in group:
            rs[g, 2].wait_recv()
            rs_end(g)
            ag[g, 0] = ag_send(g, 0)
        squares.append(sq_send(b, PIECES[group[0]][0]))
    res_store = pltpu.make_async_copy(ro_v, res_out, out_sem.at[0])
    res_store.start()
    for step in (1, 2):
        for group in (late, early):
            for g in group:
                ag[g, step - 1].wait_recv()
                ag[g, step] = ag_send(g, step)
    for copy in li_loads:
        copy.wait()
    for g in late:
        ag[g, 2].wait_recv()
    project(0, 128, squares[0])
    li_halo = send(lp.at[:, pl.ds(R, H), :], lp.at[:, pl.ds(0, H), :], halo_s.at[4], halo_r.at[4], after)
    for g in early:
        ag[g, 2].wait_recv()
    project(1, 0, squares[1])
    li_halo.wait_recv()

    li_taps = [li_short[i].astype(F32) for i in range(3)]
    for c in range(W // 128):
        lanes = slice(c * 128, (c + 1) * 128)
        three = []
        for i in range(3):
            ext = jnp.where(outside, 0.0, lp[i, :, lanes].astype(F32))
            three.append(short(ext, li_taps[i][:, lanes], R))
        ql[:, lanes] = three[0]
        ub[:, lanes] = (three[1] * three[2]).astype(BF16)
    urev[...] = jnp.dot(f512[512:, :], ub[...], preferred_element_type=F32)

    def ends(j, carry):
        for i in range(4):
            m = 4 * j + i
            st[pl.ds(m, 1), :] = jnp.sum(table[m] * urev[...], axis=0, keepdims=True)
        return carry

    lax.fori_loop(0, MODES // 4, ends, 0)
    sb[...] = st[...].astype(BF16)
    states = [
        send(sb, sr.at[k + 1], st_s.at[k], st_r.at[k], (seq_peers[k], chan)) for k in range(n_seq - 1)
    ]
    sr[0] = sb[...]

    x = jnp.dot(f512[:512, :], ub[...], preferred_element_type=F32)
    xr, xi = x[:256], x[256:]
    y = jnp.concatenate(
        [
            (xr * lt[0] - xi * lt[1]).astype(BF16),
            (xr * lt[1] + xi * lt[2]).astype(BF16),
        ],
        axis=0,
    )
    conv[...] = jnp.dot(g512[...], y, preferred_element_type=F32)

    for copy in states:
        copy.wait_recv()
    decay = jnp.exp(-rate[...] * float(R))
    zero = jnp.zeros((MODES, W), F32)
    incoming = zero
    for k in range(n_seq - 1, 0, -1):
        incoming = incoming * decay + jnp.where(seq >= k, sr[k].astype(F32), zero)
    st[...] = incoming * residue[...] * jnp.exp(-rate[...])

    def across(j, carry):
        rows = pl.ds(pl.multiple_of(j * 32, 32), 32)
        total = conv[rows, :]
        for m in range(MODES):
            total = total + st[m : m + 1, :] * table[m, rows, :]
        lo_v[rows, :] = (ql[rows, :] * total).astype(BF16)
        return carry

    lax.fori_loop(0, R // 32, across, 0)
    li_store = pltpu.make_async_copy(lo_v, li_out, out_sem.at[1])
    li_store.start()

    final = zero
    for j in range(n_seq):
        final = final * decay + sr[lax.rem(seq + n_seq - j, n_seq)].astype(F32)
    final = final * residue[...]
    high = final.astype(BF16)
    low = (final - high.astype(F32)).astype(BF16)
    mine = seq * N + chan
    block = jnp.int32(0)
    for b in range(slots.shape[0]):
        block = block + jnp.where(slots[b] == mine, jnp.int32(b), jnp.int32(0))
    source = lax.broadcasted_iota(jnp.int32, (W, W), 0) - block * CB
    target = lax.broadcasted_iota(jnp.int32, (W, W), 1) // MODES
    choose = jnp.where(source == target, 1.0, 0.0).astype(BF16)
    chosen = jnp.dot(high, choose, preferred_element_type=F32) + jnp.dot(
        low, choose, preferred_element_type=F32
    )
    m_row = lax.broadcasted_iota(jnp.int32, (MODES, W), 0)
    m_lane = lax.broadcasted_iota(jnp.int32, (MODES, W), 1) % MODES
    dec_out[...] = jnp.sum(jnp.where(m_row == m_lane, chosen, 0.0), axis=0, keepdims=True)

    for copy in pending:
        copy.wait_send()
    res_store.wait()
    li_store.wait()


def local(n_seq, residual_in, mr_query, mr_key, mr_value, mr_short, mr_filter, mix_weight, norm_gain,
          li_weight, li_short, li_rate, li_residue, decode_slot):
    f256, g256 = fourier(256, 256, 128, 128)
    f512, g512 = fourier(512, 256, 0, 256)
    f512 = np.concatenate([f512, np.eye(256)[::-1]], axis=0)
    tables = [jnp.asarray(a.astype(np.float32).astype(ml_dtypes.bfloat16)) for a in (f256, g256, f512, g512)]
    any_spec = pl.BlockSpec(memory_space=pl.ANY)
    vmem = pl.BlockSpec(memory_space=pltpu.VMEM)
    smem = pl.BlockSpec(memory_space=pltpu.SMEM)
    v = pltpu.VMEM
    dma = pltpu.SemaphoreType.DMA
    return pl.pallas_call(
        functools.partial(kernel, n_seq),
        out_shape=(
            jax.ShapeDtypeStruct((R, W), BF16),
            jax.ShapeDtypeStruct((R, W), BF16),
            jax.ShapeDtypeStruct((1, CB * MODES), F32),
        ),
        in_specs=[any_spec] * 6 + [vmem] * 6 + [smem] + [vmem] * 4,
        out_specs=(any_spec, any_spec, vmem),
        scratch_shapes=[
            v((3, H + R, W), BF16),
            v((128 + R, W), BF16),
            v((R, W), F32),
            v((3, 128, W), F32),
            v((R, W), BF16),
            v((N, W, W), BF16),
            v((2, 2, 2, R, W), BF16),
            v((2, 2, R, W), BF16),
            v((2, R, W), BF16),
            v((R, W), BF16),
            v((R, W), BF16),
            v((2, 2, 2, R, W), BF16),
            v((R, 128), F32),
            v((2, 8, 128), F32),
            v((2, N - 1, 8, 128), F32),
            v((3, N * W, W), BF16),
            v((3, H + R, W), BF16),
            v((R, W), F32),
            v((R, W), BF16),
            v((MODES, R, W), F32),
            v((R, W), F32),
            v((3, 256, W), F32),
            v((R, W), F32),
            v((R, W), F32),
            v((MODES, W), F32),
            v((MODES, W), BF16),
            v((n_seq, MODES, W), BF16),
            v((R, W), BF16),
            v((R, W), BF16),
            dma((20,)),
            dma((5,)), dma((5,)),
            dma((6, 3)), dma((6, 3)),
            dma((6, 3)), dma((6, 3)),
            dma((2, N - 1)), dma((2, N - 1)),
            dma((n_seq - 1,)), dma((n_seq - 1,)),
            dma((2,)),
        ],
        compiler_params=pltpu.CompilerParams(
            collective_id=0, has_side_effects=True, vmem_limit_bytes=60 * 1024 * 1024
        ),
        name="layers",
    )(
        residual_in, mr_query, mr_key, mr_value, mix_weight, li_weight,
        mr_short, mr_filter, norm_gain.reshape(1, W), li_short, li_rate.T, li_residue.T, decode_slot,
        *tables,
    )


def solution(mesh):
    in_specs = (
        P("seq", "chan"), P("seq", "chan"), P("seq", "chan"), P("seq", "chan"),
        P(None, None, "chan"), P(None, "chan"), P("chan", None), P("chan"),
        P(None, None, "chan"), P(None, None, "chan"), P("chan", None), P("chan", None), P("chan"),
    )
    out_specs = (P("seq", "chan"), P("seq", "chan"), P(("seq", "chan"), None))
    return jax.shard_map(
        functools.partial(local, mesh.shape["seq"]),
        mesh=mesh, in_specs=in_specs, out_specs=out_specs, check_vma=False,
    )
```

```python
import functools

import jax
import jax.numpy as jnp
import ml_dtypes
import numpy as np
from jax import lax
from jax.experimental import pallas as pl
from jax.experimental.pallas import tpu as pltpu
from jax.sharding import PartitionSpec as P

MESH = pl.DeviceIdType.MESH
F32 = jnp.float32
BF16 = jnp.bfloat16

D = 4096
MODES = 16
CB = 32
EPSILON = 1e-06
BIG = 1e30

R = 256
W = 512
H = 16
N = 8

SPLIT = 144
BATCHES = (
    ((144, 16, (0, 1, 2)), (160, 16, (1, 2, 0)), (176, 16, (2, 0, 1))),
    ((192, 32, (0, 1, 2)), (224, 16, (1, 2, 0)), (240, 16, (2, 0, 1))),
    ((0, 16, (0, 1, 2)), (16, 32, (1, 2, 0)), (48, 32, (2, 0, 1))),
    ((80, 32, (0, 1, 2)), (112, 16, (1, 2, 0)), (128, 16, (2, 0, 1))),
)
PIECES = sum(BATCHES, ())


def fourier(period, rows_in, out_from, rows_out):
    half = period // 2
    k = np.arange(half)[:, None]
    t = np.arange(rows_in)[None, :]
    angle = 2.0 * np.pi * ((k * t) % period) / period
    real, imag = np.cos(angle), -np.sin(angle)
    imag[0] = np.where(np.arange(rows_in) % 2 == 0, 1.0, -1.0)
    forward = np.concatenate([real, imag], axis=0)
    t = (out_from + np.arange(rows_out))[:, None]
    k = np.arange(half)[None, :]
    angle = 2.0 * np.pi * ((k * t) % period) / period
    real, imag = 2.0 * np.cos(angle), -2.0 * np.sin(angle)
    real[:, 0] = 1.0
    imag[:, 0] = np.where((out_from + np.arange(rows_out)) % 2 == 0, 1.0, -1.0)
    inverse = np.concatenate([real, imag], axis=1) / period
    return forward, inverse


def bits(slot):
    return (slot >> 2) & 1, (slot >> 1) & 1, slot & 1


def picked(**fixed):
    index = [slice(None)] * 3
    for name, value in fixed.items():
        index[2 - int(name[1])] = value
    return tuple(index)


def flipped(chan, slot):
    b2, b1, b0 = bits(slot)
    z, x = chan // 2, chan % 2
    if b0:
        x = 1 - x
    if b1:
        z = z + 1 - 2 * (z % 2)
    if b2:
        z = 3 - z
    return 2 * z + x


def kernel(
    n_seq,
    res_in, q_in, k_in, v_in, mix_in, liw_in, filter_in, f256_in, g256_in, f512_in, g512_in, rate_in, residue_in,
    mr_short, li_short, gain, slots,
    li_out, res_out, dec_out,
    qkv, mu, qs, ht, gated, mw, part, rb1, rb2, rb3, res_v, hb, gains, inv_gains,
    lw, lp, ql, ub, table, back, kern, lt, conv, st, sb, sr, lo_v, ro_v,
    mr_filter, f256, g256, f512, g512, rate, residue,
    load_sem, halo_s, halo_r, rs_s, rs_r, ag_s, ag_r, gain_s, gain_r, st_s, st_r, out_sem,
):
    seq, chan = lax.axis_index("seq"), lax.axis_index("chan")
    first = seq == 0
    pending = []

    loads = []

    def load(src, dst):
        copy = pltpu.make_async_copy(src, dst, load_sem.at[len(loads)])
        copy.start()
        loads.append(copy)
        return copy

    first_loads = [load(filter_in, mr_filter), load(f256_in, f256)]
    in_loads = [load(ref, qkv.at[i, pl.ds(H, R), :]) for i, ref in enumerate((q_in, k_in, v_in))]
    g_load = load(g256_in, g256)
    mix_loads = [
        load(mix_in.at[:, pl.ds(pl.multiple_of(flipped(chan, s) * W, W), W)], mw.at[s]) for s in range(N)
    ]

    barrier = pltpu.get_barrier_semaphore()
    after = (lax.rem(seq + 1, n_seq), chan)
    chan_peers = [(seq, flipped(chan, s)) for s in range(1, N)]
    seq_peers = [(lax.rem(seq + k, n_seq), chan) for k in range(1, n_seq)]
    for peer in chan_peers + seq_peers:
        pl.semaphore_signal(barrier, inc=1, device_id=peer, device_id_type=MESH)

    def send(src, dst, send_sem, recv_sem, to):
        copy = pltpu.make_async_remote_copy(
            src_ref=src, dst_ref=dst, send_sem=send_sem, recv_sem=recv_sem,
            device_id=to, device_id_type=MESH,
        )
        copy.start()
        pending.append(copy)
        return copy

    for copy in first_loads:
        copy.wait()
    spectrum = jnp.dot(f256[:, :128], mr_filter[...], preferred_element_type=F32)
    row = lax.broadcasted_iota(jnp.int32, (128, W), 0)
    ht[0] = spectrum[:128]
    ht[1] = jnp.where(row == 0, 0.0, spectrum[128:])
    ht[2] = jnp.where(row == 0, spectrum[128:], spectrum[:128])

    mode_loads = [load(rate_in, rate), load(residue_in, residue)]
    own_gain = gain[...].astype(F32).reshape(1, W)
    gains[0] = own_gain

    def short(ext, taps, rows):
        once = pltpu.roll(ext, 1, 0)
        twice = pltpu.roll(ext, 2, 0)
        top = ext.shape[0] - rows
        return taps[0:1] * ext[top:] + taps[1:2] * once[top:] + taps[2:3] * twice[top:]

    for copy in in_loads:
        copy.wait()
    mr_taps = [mr_short[i].astype(F32) for i in range(3)]
    for c in range(W // 128):
        lanes = slice(c * 128, (c + 1) * 128)
        three = [short(qkv[i, H:, lanes].astype(F32), mr_taps[i][:, lanes], R) for i in range(3)]
        qs[:, lanes] = three[0]
        mu[128:, lanes] = (three[1] * three[2]).astype(BF16)

    def filtered(r0):
        x = jnp.dot(f256[...], mu[r0 : r0 + 256, :], preferred_element_type=F32)
        xr, xi = x[:128], x[128:]
        y = jnp.concatenate(
            [
                (xr * ht[0] - xi * ht[1]).astype(BF16),
                (xr * ht[1] + xi * ht[2]).astype(BF16),
            ],
            axis=0,
        )
        return jnp.dot(g256[...], y, preferred_element_type=F32)

    def mixed(r0, r1):
        for s in range(N):
            part[bits(s) + (slice(r0, r1), slice(None))] = jnp.dot(
                gated[r0:r1, :], mw[s], preferred_element_type=F32
            ).astype(BF16)

    def fixed_bits(g, count, last=0):
        order = PIECES[g][2]
        bit = {f"b{d}": 0 for d in order[:count]}
        if last:
            bit[f"b{order[count]}"] = 1
        return picked(**bit)

    def step_send(g, step):
        r0, n, order = PIECES[g]
        rows = (pl.ds(r0, n), slice(None))
        dim = order[(0, 1, 2, 1, 0)[step]]
        to = (seq, flipped(chan, 1 << dim))
        if step < 2:
            src = part.at[fixed_bits(g, step, 1) + rows]
            dst = rb1.at[(slice(None),) * 2 + rows] if step == 0 else rb2.at[(slice(None),) + rows]
            return send(src, dst, rs_s.at[g, step], rs_r.at[g, step], to)
        if step == 2:
            src = part.at[fixed_bits(g, 2) + rows]
            return send(src, rb3.at[(slice(None),) + rows], rs_s.at[g, 2], rs_r.at[g, 2], to)
        kept = 1 if step == 3 else 0
        src = hb.at[fixed_bits(g, kept + 1) + rows]
        dst = hb.at[fixed_bits(g, kept, 1) + rows]
        return send(src, dst, ag_s.at[g, step - 3], ag_r.at[g, step - 3], to)

    def step_work(g, step):
        r0, n, order = PIECES[g]
        rows = (slice(r0, r0 + n), slice(None))
        if step == 1:
            index = fixed_bits(g, 1) + rows
            part[index] = (part[index].astype(F32) + rb1[(slice(None),) * 2 + rows].astype(F32)).astype(BF16)
        if step in (2, 3):
            near = (0, 0, 0) + rows
            far = bits(1 << order[2]) + rows
        if step == 2:
            part[near] = (
                part[near].astype(F32) + rb2[(0,) + rows].astype(F32) + res_v[rows].astype(F32)
            ).astype(BF16)
            part[far] = (part[far].astype(F32) + rb2[(1,) + rows].astype(F32)).astype(BF16)
        if step == 3:
            total = part[near].astype(F32) + rb3[(1,) + rows].astype(F32)
            ro_v[rows] = total.astype(BF16)
            hb[near] = jnp.clip(total * gains[0], -BIG, BIG).astype(BF16)
            total = part[far].astype(F32) + rb3[(0,) + rows].astype(F32)
            hb[far] = jnp.clip(total * gains[1 << order[2]], -BIG, BIG).astype(BF16)

    flying = {}

    def advance(b, step):
        for g in range(3 * b, 3 * b + 3):
            if step > 0:
                flying[g, step - 1].wait_recv()
                step_work(g, step)
            flying[g, step] = step_send(g, step)

    def row_scale(r0, r1):
        squares = jnp.zeros((r1 - r0, 128), F32)
        for s in range(N):
            sums = hb[bits(s) + (slice(r0, r1), slice(None))].astype(F32) * inv_gains[s]
            sums = sums * sums
            for c in range(W // 128):
                squares = squares + sums[:, c * 128 : (c + 1) * 128]
        return lax.rsqrt(jnp.sum(squares, axis=1, keepdims=True) / D + EPSILON)

    def project(r0, r1, inverse, which):
        lhs = jnp.concatenate([hb[bits(s) + (slice(r0, r1), slice(None))] for s in range(N)], axis=1)
        for i in which:
            out = jnp.dot(lhs, lw[i], preferred_element_type=F32) * inverse
            lp[i, H + r0 : H + r1, :] = out.astype(BF16)

    kern[...] = jnp.zeros((R, W), F32)
    time = lax.broadcasted_iota(jnp.int32, (R, W), 0).astype(F32)

    def modes(first_mode, count):
        def mode(m, carry):
            powers = jnp.exp(-rate[pl.ds(m, 1), :] * time)
            table[m] = powers
            kern[...] += residue[pl.ds(m, 1), :] * powers
            back[m] = jnp.exp(-rate[pl.ds(m, 1), :] * (R - 1.0 - time))
            return carry

        lax.fori_loop(first_mode, first_mode + count, mode, 0)

    def kernel_spectrum():
        spectrum = jnp.dot(f512[...], kern[...].astype(BF16), preferred_element_type=F32)
        row = lax.broadcasted_iota(jnp.int32, (256, W), 0)
        lt[0] = spectrum[:256]
        lt[1] = jnp.where(row == 0, 0.0, spectrum[256:])
        lt[2] = jnp.where(row == 0, spectrum[256:], spectrum[:256])

    li_taps = []

    def li_short_rows(i, r0, r1, lanes):
        ext = lp[i, r0 : H + r1, lanes].astype(F32)
        if r0 == 0:
            ext_row = lax.broadcasted_iota(jnp.int32, ext.shape, 0)
            ext = jnp.where(jnp.logical_and(first, ext_row < H), 0.0, ext)
        return short(ext, li_taps[i][:, lanes], r1 - r0)

    def li_queries(r0, r1):
        for c in range(W // 128):
            lanes = slice(c * 128, (c + 1) * 128)
            ql[r0:r1, lanes] = li_short_rows(0, r0, r1, lanes)

    def li_inputs(r0, r1):
        for c in range(W // 128):
            lanes = slice(c * 128, (c + 1) * 128)
            product = li_short_rows(1, r0, r1, lanes) * li_short_rows(2, r0, r1, lanes)
            ub[r0:r1, lanes] = product.astype(BF16)
        values = ub[r0:r1, :].astype(F32)

        def ends(j, carry):
            for i in range(4):
                m = 4 * j + i
                st[pl.ds(m, 1), :] += jnp.sum(back[m, r0:r1, :] * values, axis=0, keepdims=True)
            return carry

        lax.fori_loop(0, MODES // 4, ends, 0)

    g_load.wait()
    out = filtered(128)
    gated[SPLIT:, :] = (qs[SPLIT:, :] * out[SPLIT - 128 :]).astype(BF16)
    pl.semaphore_wait(barrier, N - 1 + n_seq - 1)
    halos = [
        send(qkv.at[i, pl.ds(R, H), :], qkv.at[i, pl.ds(0, H), :], halo_s.at[i], halo_r.at[i], after)
        for i in range(3)
    ]
    rim = send(mu.at[pl.ds(R, 128), :], mu.at[pl.ds(0, 128), :], halo_s.at[3], halo_r.at[3], after)
    for copy in mix_loads:
        copy.wait()
    mixed(SPLIT, 192)
    advance(0, 0)
    mixed(192, R)
    advance(1, 0)

    gain_sends = [
        send(gains.at[0], gains.at[s], gain_s.at[s - 1], gain_r.at[s - 1], chan_peers[s - 1])
        for s in range(1, N)
    ]
    res_load = load(res_in, res_v)
    more_loads = [load(f512_in, f512), load(g512_in, g512)]
    li_loads = [
        load(liw_in.at[:, pl.ds(pl.multiple_of(flipped(chan, s) * W, W), W), :], lw.at[:, pl.ds(s * W, W), :])
        for s in range(N)
    ]
    for copy in mode_loads:
        copy.wait()
    modes(0, 4)

    advance(0, 1)

    for copy in halos:
        copy.wait_recv()
    fixed = []
    ext_row = lax.broadcasted_iota(jnp.int32, (2 * H, W), 0)
    outside = jnp.logical_and(first, ext_row < H)
    for i in range(3):
        ext = jnp.where(outside, 0.0, qkv[i, : 2 * H, :].astype(F32))
        fixed.append(short(ext, mr_taps[i], H))
    qs[:H, :] = fixed[0]
    right = (fixed[1] * fixed[2]).astype(BF16)
    missed = (right.astype(F32) - mu[128 : 128 + H, :].astype(F32))[1:2] * mr_filter[127:128, :].astype(F32)
    mu[128 : 128 + H, :] = right
    ahead = out[: SPLIT - 128]
    ahead = ahead + jnp.where(lax.broadcasted_iota(jnp.int32, ahead.shape, 0) == 0, missed, 0.0)
    gated[128:SPLIT, :] = (qs[128:SPLIT, :] * ahead).astype(BF16)
    rim.wait_recv()
    mu[:128, :] = jnp.where(first, jnp.zeros((128, W), BF16), mu[:128, :])
    gated[:128, :] = (qs[:128, :] * filtered(0)).astype(BF16)
    mixed(0, 80)
    advance(2, 0)
    mixed(80, SPLIT)
    advance(3, 0)

    advance(1, 1)
    modes(4, 4)
    res_load.wait()
    for copy in gain_sends:
        copy.wait_recv()
    for s in range(N):
        inv_gains[s] = 1.0 / gains[s]
    advance(0, 2)
    modes(8, 4)
    advance(2, 1)
    advance(3, 1)
    advance(1, 2)
    advance(0, 3)
    modes(12, 4)
    advance(2, 2)
    advance(3, 2)
    advance(1, 3)
    advance(0, 4)
    for copy in more_loads:
        copy.wait()
    kernel_spectrum()
    advance(2, 3)
    advance(3, 3)
    advance(1, 4)
    res_store = pltpu.make_async_copy(ro_v, res_out, out_sem.at[0])
    res_store.start()
    for copy in li_loads:
        copy.wait()
    li_taps.extend(li_short[i].astype(F32) for i in range(3))
    st[...] = jnp.zeros((MODES, W), F32)
    advance(2, 4)
    advance(3, 4)

    def arrived(*batches):
        for b in batches:
            for g in range(3 * b, 3 * b + 3):
                flying[g, 4].wait_recv()

    arrived(0, 1)
    project(SPLIT, R, row_scale(SPLIT, R), (0, 1, 2))
    li_halo = send(lp.at[:, pl.ds(R, H), :], lp.at[:, pl.ds(0, H), :], halo_s.at[4], halo_r.at[4], after)
    li_inputs(160, R)
    li_queries(160, R)
    arrived(2, 3)
    inverse = row_scale(0, SPLIT)
    project(0, SPLIT, inverse, (1, 2))
    li_halo.wait_recv()
    li_inputs(0, 160)
    sb[...] = st[...].astype(BF16)
    states = [send(sb, sr.at[k + 1], st_s.at[k], st_r.at[k], seq_peers[k]) for k in range(n_seq - 1)]
    project(0, SPLIT, inverse, (0,))
    li_queries(0, 160)

    x = jnp.dot(f512[...], ub[...], preferred_element_type=F32)
    xr, xi = x[:256], x[256:]
    y = jnp.concatenate(
        [
            (xr * lt[0] - xi * lt[1]).astype(BF16),
            (xr * lt[1] + xi * lt[2]).astype(BF16),
        ],
        axis=0,
    )
    conv[...] = jnp.dot(g512[...], y, preferred_element_type=F32)

    sr[0] = sb[...]
    decay = jnp.exp(-rate[...] * float(R))
    leaving = residue[...] * jnp.exp(-rate[...])
    for copy in states:
        copy.wait_recv()
    incoming = jnp.zeros((MODES, W), F32)
    for k in range(n_seq - 1, 0, -1):
        incoming = incoming * decay + jnp.where(seq >= k, sr[k].astype(F32), 0.0)
    st[...] = incoming * leaving

    def across(j, carry):
        rows = pl.ds(pl.multiple_of(j * 32, 32), 32)
        total = conv[rows, :]
        for m in range(MODES):
            total = total + st[m : m + 1, :] * table[m, rows, :]
        lo_v[rows, :] = (ql[rows, :] * total).astype(BF16)
        return carry

    stores = [res_store]
    for i in range(2):
        lax.fori_loop(i * R // 64, (i + 1) * R // 64, across, 0)
        rows = pl.ds(i * (R // 2), R // 2)
        stores.append(pltpu.make_async_copy(lo_v.at[rows, :], li_out.at[rows, :], out_sem.at[1 + i]))
        stores[-1].start()

    final = jnp.zeros((MODES, W), F32)
    for j in range(n_seq):
        final = final * decay + sr[lax.rem(seq + n_seq - j, n_seq)].astype(F32)
    final = final * residue[...]
    high = final.astype(BF16)
    low = (final - high.astype(F32)).astype(BF16)
    mine = seq * N + chan
    block = jnp.int32(0)
    for b in range(slots.shape[0]):
        block = block + jnp.where(slots[b] == mine, jnp.int32(b), jnp.int32(0))
    source = lax.broadcasted_iota(jnp.int32, (W, W), 0) - block * CB
    target = lax.broadcasted_iota(jnp.int32, (W, W), 1) // MODES
    choose = jnp.where(source == target, 1.0, 0.0).astype(BF16)
    chosen = jnp.dot(high, choose, preferred_element_type=F32) + jnp.dot(
        low, choose, preferred_element_type=F32
    )
    m_row = lax.broadcasted_iota(jnp.int32, (MODES, W), 0)
    m_lane = lax.broadcasted_iota(jnp.int32, (MODES, W), 1) % MODES
    dec_out[...] = jnp.sum(jnp.where(m_row == m_lane, chosen, 0.0), axis=0, keepdims=True)

    for copy in pending:
        copy.wait_send()
    for copy in stores:
        copy.wait()


def hand_over(li_in, res_in, dec_in, li_out, res_out, dec_out, li_v, res_v, dec_v, sem):
    trips = ((li_in, li_v, li_out), (res_in, res_v, res_out), (dec_in, dec_v, dec_out))
    there = [pltpu.make_async_copy(src, held, sem.at[0, i]) for i, (src, held, _) in enumerate(trips)]
    again = [pltpu.make_async_copy(held, dst, sem.at[1, i]) for i, (_, held, dst) in enumerate(trips)]
    for copy in there:
        copy.start()
    for copy, later in zip(there, again):
        copy.wait()
        later.start()
    for copy in again:
        copy.wait()


def local(n_seq, residual_in, mr_query, mr_key, mr_value, mr_short, mr_filter, mix_weight, norm_gain,
          li_weight, li_short, li_rate, li_residue, decode_slot):
    f256, g256 = fourier(256, 256, 128, 128)
    f512, g512 = fourier(512, 256, 0, 256)
    tables = [jnp.asarray(a.astype(np.float32).astype(ml_dtypes.bfloat16)) for a in (f256, g256, f512, g512)]
    hbm = pl.BlockSpec(memory_space=pltpu.HBM)
    vmem = pl.BlockSpec(memory_space=pltpu.VMEM)
    smem = pl.BlockSpec(memory_space=pltpu.SMEM)
    v = pltpu.VMEM
    dma = pltpu.SemaphoreType.DMA
    shapes = (
        jax.ShapeDtypeStruct((R, W), BF16),
        jax.ShapeDtypeStruct((R, W), BF16),
        jax.ShapeDtypeStruct((1, CB * MODES), F32),
    )
    done = pl.pallas_call(
        functools.partial(kernel, n_seq),
        out_shape=shapes,
        in_specs=[hbm] * 13 + [vmem] * 3 + [smem],
        out_specs=(hbm, hbm, vmem),
        scratch_shapes=[
            v((3, H + R, W), BF16),
            v((128 + R, W), BF16),
            v((R, W), F32),
            v((3, 128, W), F32),
            v((R, W), BF16),
            v((N, W, W), BF16),
            v((2, 2, 2, R, W), BF16),
            v((2, 2, R, W), BF16),
            v((2, R, W), BF16),
            v((2, R, W), BF16),
            v((R, W), BF16),
            v((2, 2, 2, R, W), BF16),
            v((N, 1, W), F32),
            v((N, 1, W), F32),
            v((3, N * W, W), BF16),
            v((3, H + R, W), BF16),
            v((R, W), F32),
            v((R, W), BF16),
            v((MODES, R, W), F32),
            v((MODES, R, W), F32),
            v((R, W), F32),
            v((3, 256, W), F32),
            v((R, W), F32),
            v((MODES, W), F32),
            v((MODES, W), BF16),
            v((n_seq, MODES, W), BF16),
            v((R, W), BF16),
            v((R, W), BF16),
            v((128, W), BF16),
            v((256, 256), BF16),
            v((128, 256), BF16),
            v((512, 256), BF16),
            v((256, 512), BF16),
            v((MODES, W), F32),
            v((MODES, W), F32),
            dma((30,)),
            dma((5,)), dma((5,)),
            dma((len(PIECES), 3)), dma((len(PIECES), 3)),
            dma((len(PIECES), 2)), dma((len(PIECES), 2)),
            dma((N - 1,)), dma((N - 1,)),
            dma((n_seq - 1,)), dma((n_seq - 1,)),
            dma((3,)),
        ],
        compiler_params=pltpu.CompilerParams(
            collective_id=0, has_side_effects=True, vmem_limit_bytes=60 * 1024 * 1024
        ),
        name="layers",
    )(
        residual_in, mr_query, mr_key, mr_value, mix_weight, li_weight, mr_filter, *tables, li_rate.T, li_residue.T,
        mr_short, li_short, norm_gain, decode_slot,
    )
    return pl.pallas_call(
        hand_over,
        out_shape=shapes,
        in_specs=[hbm] * 3,
        out_specs=(hbm,) * 3,
        scratch_shapes=[v((R, W), BF16), v((R, W), BF16), v((1, CB * MODES), F32), dma((2, 3))],
        compiler_params=pltpu.CompilerParams(vmem_limit_bytes=60 * 1024 * 1024),
        name="hand_over",
    )(*done)


def solution(mesh):
    in_specs = (
        P("seq", "chan"), P("seq", "chan"), P("seq", "chan"), P("seq", "chan"),
        P(None, None, "chan"), P(None, "chan"), P("chan", None), P("chan"),
        P(None, None, "chan"), P(None, None, "chan"), P("chan", None), P("chan", None), P("chan"),
    )
    out_specs = (P("seq", "chan"), P("seq", "chan"), P(("seq", "chan"), None))
    return jax.shard_map(
        functools.partial(local, mesh.shape["seq"]),
        mesh=mesh, in_specs=in_specs, out_specs=out_specs, check_vma=False,
    )
```

```python
import functools

import jax
import jax.numpy as jnp
import ml_dtypes
import numpy as np
from jax import lax
from jax.experimental import pallas as pl
from jax.experimental.pallas import tpu as pltpu
from jax.sharding import PartitionSpec as P

MESH = pl.DeviceIdType.MESH
F32 = jnp.float32
BF16 = jnp.bfloat16

D = 4096
MODES = 16
CB = 32
EPSILON = 1e-06
BIG = 1e30

R = 256
W = 512
H = 16
N = 8

SPLIT = 144
BATCHES = (
    ((144, 16, (0, 1, 2)), (160, 16, (1, 2, 0)), (176, 16, (2, 0, 1))),
    ((192, 32, (0, 1, 2)), (224, 16, (1, 2, 0)), (240, 16, (2, 0, 1))),
    ((0, 16, (0, 1, 2)), (16, 32, (1, 2, 0)), (48, 32, (2, 0, 1))),
    ((80, 32, (0, 1, 2)), (112, 16, (1, 2, 0)), (128, 16, (2, 0, 1))),
)
PIECES = sum(BATCHES, ())


def fourier(period, rows_in, out_from, rows_out):
    half = period // 2
    k = np.arange(half)[:, None]
    t = np.arange(rows_in)[None, :]
    angle = 2.0 * np.pi * ((k * t) % period) / period
    real, imag = np.cos(angle), -np.sin(angle)
    imag[0] = np.where(np.arange(rows_in) % 2 == 0, 1.0, -1.0)
    forward = np.concatenate([real, imag], axis=0)
    t = (out_from + np.arange(rows_out))[:, None]
    k = np.arange(half)[None, :]
    angle = 2.0 * np.pi * ((k * t) % period) / period
    real, imag = 2.0 * np.cos(angle), -2.0 * np.sin(angle)
    real[:, 0] = 1.0
    imag[:, 0] = np.where((out_from + np.arange(rows_out)) % 2 == 0, 1.0, -1.0)
    inverse = np.concatenate([real, imag], axis=1) / period
    return forward, inverse


def bits(slot):
    return (slot >> 2) & 1, (slot >> 1) & 1, slot & 1


def picked(**fixed):
    index = [slice(None)] * 3
    for name, value in fixed.items():
        index[2 - int(name[1])] = value
    return tuple(index)


def flipped(chan, slot):
    b2, b1, b0 = bits(slot)
    z, x = chan // 2, chan % 2
    if b0:
        x = 1 - x
    if b1:
        z = z + 1 - 2 * (z % 2)
    if b2:
        z = 3 - z
    return 2 * z + x


def kernel(
    n_seq,
    res_in, q_in, k_in, v_in, mix_in, liw_in, filter_in, f256_in, g256_in, f512_in, g512_in, rate_in, residue_in,
    mr_short_in, li_short_in, gain_in, slots_in,
    li_out, res_out, dec_out,
    qkv, mu, qs, ht, gated, mw, part, rb1, rb2, rb3, res_v, hb, gains, inv_gains,
    lw, lp, ql, ub, table, back, kern, lt, conv, st, sb, sr, lo_v, ro_v,
    mr_filter, f256, g256, f512, g512, rate, residue, mr_short, li_short, gain, slots,
    load_sem, halo_s, halo_r, rs_s, rs_r, ag_s, ag_r, gain_s, gain_r, st_s, st_r, out_sem,
):
    seq, chan = lax.axis_index("seq"), lax.axis_index("chan")
    first = seq == 0
    pending = []

    barrier = pltpu.get_barrier_semaphore()
    after = (lax.rem(seq + 1, n_seq), chan)
    chan_peers = [(seq, flipped(chan, s)) for s in range(1, N)]
    seq_peers = [(lax.rem(seq + k, n_seq), chan) for k in range(1, n_seq)]
    for peer in chan_peers + seq_peers:
        pl.semaphore_signal(barrier, inc=1, device_id=peer, device_id_type=MESH)

    loads = []

    def load(src, dst):
        copy = pltpu.make_async_copy(src, dst, load_sem.at[len(loads)])
        copy.start()
        loads.append(copy)
        return copy

    first_loads = [load(filter_in, mr_filter), load(f256_in, f256)]
    in_loads = [load(mr_short_in, mr_short)] + [
        load(ref, qkv.at[i, pl.ds(H, R), :]) for i, ref in enumerate((q_in, k_in, v_in))
    ]
    g_load = load(g256_in, g256)
    mix_loads = [
        load(mix_in.at[:, pl.ds(pl.multiple_of(flipped(chan, s) * W, W), W)], mw.at[s]) for s in range(N)
    ]

    def remote(src, dst, send_sem, recv_sem, to):
        return pltpu.make_async_remote_copy(
            src_ref=src, dst_ref=dst, send_sem=send_sem, recv_sem=recv_sem,
            device_id=to, device_id_type=MESH,
        )

    def send(*what):
        copy = remote(*what)
        copy.start()
        pending.append(copy)
        return copy

    def hand_on(*copies):
        @pl.when(seq < n_seq - 1)
        def _():
            for copy in copies:
                copy.start()

    def handed(*copies):
        @pl.when(seq > 0)
        def _():
            for copy in copies:
                copy.wait_recv()

    def handed_on(*copies):
        @pl.when(seq < n_seq - 1)
        def _():
            for copy in copies:
                copy.wait_send()

    for copy in first_loads:
        copy.wait()
    spectrum = jnp.dot(f256[:, :128], mr_filter[...], preferred_element_type=F32)
    row = lax.broadcasted_iota(jnp.int32, (128, W), 0)
    ht[0] = spectrum[:128]
    ht[1] = jnp.where(row == 0, 0.0, spectrum[128:])
    ht[2] = jnp.where(row == 0, spectrum[128:], spectrum[:128])

    gain_load = load(gain_in, gain)
    mode_loads = [load(rate_in, rate), load(residue_in, residue)]

    def short(ext, taps, rows):
        once = pltpu.roll(ext, 1, 0)
        twice = pltpu.roll(ext, 2, 0)
        top = ext.shape[0] - rows
        return taps[0:1] * ext[top:] + taps[1:2] * once[top:] + taps[2:3] * twice[top:]

    for copy in in_loads:
        copy.wait()
    mr_taps = [mr_short[i].astype(F32) for i in range(3)]
    for c in range(W // 128):
        lanes = slice(c * 128, (c + 1) * 128)
        three = [short(qkv[i, H:, lanes].astype(F32), mr_taps[i][:, lanes], R) for i in range(3)]
        qs[:, lanes] = three[0]
        mu[128:, lanes] = (three[1] * three[2]).astype(BF16)

    def filtered(r0):
        x = jnp.dot(f256[...], mu[r0 : r0 + 256, :], preferred_element_type=F32)
        xr, xi = x[:128], x[128:]
        y = jnp.concatenate(
            [
                (xr * ht[0] - xi * ht[1]).astype(BF16),
                (xr * ht[1] + xi * ht[2]).astype(BF16),
            ],
            axis=0,
        )
        return jnp.dot(g256[...], y, preferred_element_type=F32)

    def mixed(r0, r1):
        for s in range(N):
            part[bits(s) + (slice(r0, r1), slice(None))] = jnp.dot(
                gated[r0:r1, :], mw[s], preferred_element_type=F32
            ).astype(BF16)

    def fixed_bits(g, count, last=0):
        order = PIECES[g][2]
        bit = {f"b{d}": 0 for d in order[:count]}
        if last:
            bit[f"b{order[count]}"] = 1
        return picked(**bit)

    def step_send(g, step):
        r0, n, order = PIECES[g]
        rows = (pl.ds(r0, n), slice(None))
        dim = order[(0, 1, 2, 1, 0)[step]]
        to = (seq, flipped(chan, 1 << dim))
        if step < 2:
            src = part.at[fixed_bits(g, step, 1) + rows]
            dst = rb1.at[(slice(None),) * 2 + rows] if step == 0 else rb2.at[(slice(None),) + rows]
            return send(src, dst, rs_s.at[g, step], rs_r.at[g, step], to)
        if step == 2:
            src = part.at[fixed_bits(g, 2) + rows]
            return send(src, rb3.at[(slice(None),) + rows], rs_s.at[g, 2], rs_r.at[g, 2], to)
        kept = 1 if step == 3 else 0
        src = hb.at[fixed_bits(g, kept + 1) + rows]
        dst = hb.at[fixed_bits(g, kept, 1) + rows]
        return send(src, dst, ag_s.at[g, step - 3], ag_r.at[g, step - 3], to)

    def step_work(g, step):
        r0, n, order = PIECES[g]
        rows = (slice(r0, r0 + n), slice(None))
        if step == 1:
            index = fixed_bits(g, 1) + rows
            part[index] = (part[index].astype(F32) + rb1[(slice(None),) * 2 + rows].astype(F32)).astype(BF16)
        if step in (2, 3):
            near = (0, 0, 0) + rows
            far = bits(1 << order[2]) + rows
        if step == 2:
            part[near] = (
                part[near].astype(F32) + rb2[(0,) + rows].astype(F32) + res_v[rows].astype(F32)
            ).astype(BF16)
            part[far] = (part[far].astype(F32) + rb2[(1,) + rows].astype(F32)).astype(BF16)
        if step == 3:
            total = part[near].astype(F32) + rb3[(1,) + rows].astype(F32)
            ro_v[rows] = total.astype(BF16)
            hb[near] = jnp.clip(total * gains[0], -BIG, BIG).astype(BF16)
            total = part[far].astype(F32) + rb3[(0,) + rows].astype(F32)
            hb[far] = jnp.clip(total * gains[1 << order[2]], -BIG, BIG).astype(BF16)

    flying = {}

    def advance(b, step):
        for g in range(3 * b, 3 * b + 3):
            if step > 0:
                flying[g, step - 1].wait_recv()
                step_work(g, step)
            flying[g, step] = step_send(g, step)

    def row_scale(r0, r1):
        squares = jnp.zeros((r1 - r0, 128), F32)
        for s in range(N):
            sums = hb[bits(s) + (slice(r0, r1), slice(None))].astype(F32) * inv_gains[s]
            sums = sums * sums
            for c in range(W // 128):
                squares = squares + sums[:, c * 128 : (c + 1) * 128]
        return lax.rsqrt(jnp.sum(squares, axis=1, keepdims=True) / D + EPSILON)

    def project(r0, r1, inverse, which):
        lhs = jnp.concatenate([hb[bits(s) + (slice(r0, r1), slice(None))] for s in range(N)], axis=1)
        for i in which:
            out = jnp.dot(lhs, lw[i], preferred_element_type=F32) * inverse
            lp[i, H + r0 : H + r1, :] = out.astype(BF16)

    kern[...] = jnp.zeros((R, W), F32)
    time = lax.broadcasted_iota(jnp.int32, (R, W), 0).astype(F32)

    def modes(first_mode, count):
        def mode(m, carry):
            powers = jnp.exp(-rate[pl.ds(m, 1), :] * time)
            table[m] = powers
            kern[...] += residue[pl.ds(m, 1), :] * powers
            back[m] = jnp.exp(-rate[pl.ds(m, 1), :] * (R - 1.0 - time))
            return carry

        lax.fori_loop(first_mode, first_mode + count, mode, 0)

    def kernel_spectrum():
        spectrum = jnp.dot(f512[...], kern[...].astype(BF16), preferred_element_type=F32)
        row = lax.broadcasted_iota(jnp.int32, (256, W), 0)
        lt[0] = spectrum[:256]
        lt[1] = jnp.where(row == 0, 0.0, spectrum[256:])
        lt[2] = jnp.where(row == 0, spectrum[256:], spectrum[:256])

    li_taps = []

    def li_short_rows(i, r0, r1, lanes):
        ext = lp[i, r0 : H + r1, lanes].astype(F32)
        if r0 == 0:
            ext_row = lax.broadcasted_iota(jnp.int32, ext.shape, 0)
            ext = jnp.where(jnp.logical_and(first, ext_row < H), 0.0, ext)
        return short(ext, li_taps[i][:, lanes], r1 - r0)

    def li_queries(r0, r1):
        for c in range(W // 128):
            lanes = slice(c * 128, (c + 1) * 128)
            ql[r0:r1, lanes] = li_short_rows(0, r0, r1, lanes)

    def li_inputs(r0, r1):
        for c in range(W // 128):
            lanes = slice(c * 128, (c + 1) * 128)
            product = li_short_rows(1, r0, r1, lanes) * li_short_rows(2, r0, r1, lanes)
            ub[r0:r1, lanes] = product.astype(BF16)
        values = ub[r0:r1, :].astype(F32)

        def ends(j, carry):
            for i in range(4):
                m = 4 * j + i
                st[pl.ds(m, 1), :] += jnp.sum(back[m, r0:r1, :] * values, axis=0, keepdims=True)
            return carry

        lax.fori_loop(0, MODES // 4, ends, 0)

    g_load.wait()
    out = filtered(128)
    gated[SPLIT:, :] = (qs[SPLIT:, :] * out[SPLIT - 128 :]).astype(BF16)
    for copy in mix_loads:
        copy.wait()
    mixed(SPLIT, 192)
    pl.semaphore_wait(barrier, N - 1 + n_seq - 1)
    halos = [
        remote(qkv.at[i, pl.ds(R, H), :], qkv.at[i, pl.ds(0, H), :], halo_s.at[i], halo_r.at[i], after)
        for i in range(3)
    ]
    rim = remote(mu.at[pl.ds(R, 128), :], mu.at[pl.ds(0, 128), :], halo_s.at[3], halo_r.at[3], after)
    hand_on(*halos, rim)
    advance(0, 0)
    mixed(192, R)
    advance(1, 0)

    gain_load.wait()
    gains[0] = gain[...].astype(F32).reshape(1, W)
    gain_sends = [
        send(gains.at[0], gains.at[s], gain_s.at[s - 1], gain_r.at[s - 1], chan_peers[s - 1])
        for s in range(1, N)
    ]
    res_load = load(res_in, res_v)
    more_loads = [load(f512_in, f512), load(g512_in, g512), load(li_short_in, li_short), load(slots_in, slots)]
    li_loads = [
        load(liw_in.at[:, pl.ds(pl.multiple_of(flipped(chan, s) * W, W), W), :], lw.at[:, pl.ds(s * W, W), :])
        for s in range(N)
    ]
    for copy in mode_loads:
        copy.wait()
    modes(0, 4)

    advance(0, 1)

    handed(*halos)
    fixed = []
    ext_row = lax.broadcasted_iota(jnp.int32, (2 * H, W), 0)
    outside = jnp.logical_and(first, ext_row < H)
    for i in range(3):
        ext = jnp.where(outside, 0.0, qkv[i, : 2 * H, :].astype(F32))
        fixed.append(short(ext, mr_taps[i], H))
    qs[:H, :] = fixed[0]
    right = (fixed[1] * fixed[2]).astype(BF16)
    missed = (right.astype(F32) - mu[128 : 128 + H, :].astype(F32))[1:2] * mr_filter[127:128, :].astype(F32)
    mu[128 : 128 + H, :] = right
    ahead = out[: SPLIT - 128]
    ahead = ahead + jnp.where(lax.broadcasted_iota(jnp.int32, ahead.shape, 0) == 0, missed, 0.0)
    gated[128:SPLIT, :] = (qs[128:SPLIT, :] * ahead).astype(BF16)
    handed(rim)
    mu[:128, :] = jnp.where(first, jnp.zeros((128, W), BF16), mu[:128, :])
    gated[:128, :] = (qs[:128, :] * filtered(0)).astype(BF16)
    mixed(0, 80)
    advance(2, 0)
    mixed(80, SPLIT)
    advance(3, 0)

    advance(1, 1)
    modes(4, 4)
    res_load.wait()
    for copy in gain_sends:
        copy.wait_recv()
    for s in range(N):
        inv_gains[s] = 1.0 / gains[s]
    advance(0, 2)
    modes(8, 4)
    advance(2, 1)
    advance(3, 1)
    advance(1, 2)
    advance(0, 3)
    modes(12, 4)
    advance(2, 2)
    advance(3, 2)
    advance(1, 3)
    advance(0, 4)
    for copy in more_loads:
        copy.wait()
    kernel_spectrum()
    advance(2, 3)
    advance(3, 3)
    advance(1, 4)
    res_store = pltpu.make_async_copy(ro_v, res_out, out_sem.at[0])
    res_store.start()
    for copy in li_loads:
        copy.wait()
    li_taps.extend(li_short[i].astype(F32) for i in range(3))
    st[...] = jnp.zeros((MODES, W), F32)
    advance(2, 4)
    advance(3, 4)

    def arrived(*batches):
        for b in batches:
            for g in range(3 * b, 3 * b + 3):
                flying[g, 4].wait_recv()

    arrived(0, 1)
    project(SPLIT, R, row_scale(SPLIT, R), (0, 1, 2))
    li_halo = remote(lp.at[:, pl.ds(R, H), :], lp.at[:, pl.ds(0, H), :], halo_s.at[4], halo_r.at[4], after)
    hand_on(li_halo)
    li_inputs(160, R)
    li_queries(160, R)
    arrived(2, 3)
    inverse = row_scale(0, SPLIT)
    project(0, SPLIT, inverse, (1, 2))
    handed(li_halo)
    li_inputs(0, 160)
    sb[...] = st[...].astype(BF16)
    states = [send(sb, sr.at[k + 1], st_s.at[k], st_r.at[k], seq_peers[k]) for k in range(n_seq - 1)]
    project(0, SPLIT, inverse, (0,))
    li_queries(0, 160)

    x = jnp.dot(f512[...], ub[...], preferred_element_type=F32)
    xr, xi = x[:256], x[256:]
    y = jnp.concatenate(
        [
            (xr * lt[0] - xi * lt[1]).astype(BF16),
            (xr * lt[1] + xi * lt[2]).astype(BF16),
        ],
        axis=0,
    )
    conv[...] = jnp.dot(g512[...], y, preferred_element_type=F32)

    sr[0] = sb[...]
    decay = jnp.exp(-rate[...] * float(R))
    leaving = residue[...] * jnp.exp(-rate[...])
    for copy in states:
        copy.wait_recv()
    incoming = jnp.zeros((MODES, W), F32)
    for k in range(n_seq - 1, 0, -1):
        incoming = incoming * decay + jnp.where(seq >= k, sr[k].astype(F32), 0.0)
    st[...] = incoming * leaving

    def across(j, carry):
        rows = pl.ds(pl.multiple_of(j * 32, 32), 32)
        total = conv[rows, :]
        for m in range(MODES):
            total = total + st[m : m + 1, :] * table[m, rows, :]
        lo_v[rows, :] = (ql[rows, :] * total).astype(BF16)
        return carry

    stores = [res_store]
    for i in range(2):
        lax.fori_loop(i * R // 64, (i + 1) * R // 64, across, 0)
        rows = pl.ds(i * (R // 2), R // 2)
        stores.append(pltpu.make_async_copy(lo_v.at[rows, :], li_out.at[rows, :], out_sem.at[1 + i]))
        stores[-1].start()

    final = jnp.zeros((MODES, W), F32)
    for j in range(n_seq):
        final = final * decay + sr[lax.rem(seq + n_seq - j, n_seq)].astype(F32)
    final = final * residue[...]
    high = final.astype(BF16)
    low = (final - high.astype(F32)).astype(BF16)
    mine = seq * N + chan
    block = jnp.int32(0)
    for b in range(slots.shape[0]):
        block = block + jnp.where(slots[b] == mine, jnp.int32(b), jnp.int32(0))
    source = lax.broadcasted_iota(jnp.int32, (W, W), 0) - block * CB
    target = lax.broadcasted_iota(jnp.int32, (W, W), 1) // MODES
    choose = jnp.where(source == target, 1.0, 0.0).astype(BF16)
    chosen = jnp.dot(high, choose, preferred_element_type=F32) + jnp.dot(
        low, choose, preferred_element_type=F32
    )
    m_row = lax.broadcasted_iota(jnp.int32, (MODES, W), 0)
    m_lane = lax.broadcasted_iota(jnp.int32, (MODES, W), 1) % MODES
    dec_out[...] = jnp.sum(jnp.where(m_row == m_lane, chosen, 0.0), axis=0, keepdims=True)

    handed_on(*halos, rim, li_halo)
    for copy in pending:
        copy.wait_send()
    for copy in stores:
        copy.wait()


def hand_over(li_in, res_in, dec_in, li_out, res_out, dec_out, li_v, res_v, dec_v, sem):
    trips = ((li_in, li_v, li_out), (res_in, res_v, res_out), (dec_in, dec_v, dec_out))
    there = [pltpu.make_async_copy(src, held, sem.at[0, i]) for i, (src, held, _) in enumerate(trips)]
    again = [pltpu.make_async_copy(held, dst, sem.at[1, i]) for i, (_, held, dst) in enumerate(trips)]
    for copy in there:
        copy.start()
    for copy, later in zip(there, again):
        copy.wait()
        later.start()
    for copy in again:
        copy.wait()


def local(n_seq, residual_in, mr_query, mr_key, mr_value, mr_short, mr_filter, mix_weight, norm_gain,
          li_weight, li_short, li_rate, li_residue, decode_slot):
    f256, g256 = fourier(256, 256, 128, 128)
    f512, g512 = fourier(512, 256, 0, 256)
    tables = [jnp.asarray(a.astype(np.float32).astype(ml_dtypes.bfloat16)) for a in (f256, g256, f512, g512)]
    hbm = pl.BlockSpec(memory_space=pltpu.HBM)
    vmem = pl.BlockSpec(memory_space=pltpu.VMEM)
    v = pltpu.VMEM
    dma = pltpu.SemaphoreType.DMA
    shapes = (
        jax.ShapeDtypeStruct((R, W), BF16),
        jax.ShapeDtypeStruct((R, W), BF16),
        jax.ShapeDtypeStruct((1, CB * MODES), F32),
    )
    done = pl.pallas_call(
        functools.partial(kernel, n_seq),
        out_shape=shapes,
        in_specs=[hbm] * 17,
        out_specs=(hbm, hbm, vmem),
        scratch_shapes=[
            v((3, H + R, W), BF16),
            v((128 + R, W), BF16),
            v((R, W), F32),
            v((3, 128, W), F32),
            v((R, W), BF16),
            v((N, W, W), BF16),
            v((2, 2, 2, R, W), BF16),
            v((2, 2, R, W), BF16),
            v((2, R, W), BF16),
            v((2, R, W), BF16),
            v((R, W), BF16),
            v((2, 2, 2, R, W), BF16),
            v((N, 1, W), F32),
            v((N, 1, W), F32),
            v((3, N * W, W), BF16),
            v((3, H + R, W), BF16),
            v((R, W), F32),
            v((R, W), BF16),
            v((MODES, R, W), F32),
            v((MODES, R, W), F32),
            v((R, W), F32),
            v((3, 256, W), F32),
            v((R, W), F32),
            v((MODES, W), F32),
            v((MODES, W), BF16),
            v((n_seq, MODES, W), BF16),
            v((R, W), BF16),
            v((R, W), BF16),
            v((128, W), BF16),
            v((256, 256), BF16),
            v((128, 256), BF16),
            v((512, 256), BF16),
            v((256, 512), BF16),
            v((MODES, W), F32),
            v((MODES, W), F32),
            v((3, 3, W), BF16),
            v((3, 3, W), BF16),
            v((W,), BF16),
            pltpu.SMEM((16,), jnp.int32),
            dma((31,)),
            dma((5,)), dma((5,)),
            dma((len(PIECES), 3)), dma((len(PIECES), 3)),
            dma((len(PIECES), 2)), dma((len(PIECES), 2)),
            dma((N - 1,)), dma((N - 1,)),
            dma((n_seq - 1,)), dma((n_seq - 1,)),
            dma((3,)),
        ],
        compiler_params=pltpu.CompilerParams(
            collective_id=0, has_side_effects=True, vmem_limit_bytes=60 * 1024 * 1024
        ),
        name="layers",
    )(
        residual_in, mr_query, mr_key, mr_value, mix_weight, li_weight, mr_filter, *tables, li_rate.T, li_residue.T,
        mr_short, li_short, norm_gain, decode_slot,
    )
    return pl.pallas_call(
        hand_over,
        out_shape=shapes,
        in_specs=[hbm] * 3,
        out_specs=(hbm,) * 3,
        scratch_shapes=[v((R, W), BF16), v((R, W), BF16), v((1, CB * MODES), F32), dma((2, 3))],
        compiler_params=pltpu.CompilerParams(vmem_limit_bytes=60 * 1024 * 1024),
        name="hand_over",
    )(*done)


def solution(mesh):
    in_specs = (
        P("seq", "chan"), P("seq", "chan"), P("seq", "chan"), P("seq", "chan"),
        P(None, None, "chan"), P(None, "chan"), P("chan", None), P("chan"),
        P(None, None, "chan"), P(None, None, "chan"), P("chan", None), P("chan", None), P("chan"),
    )
    out_specs = (P("seq", "chan"), P("seq", "chan"), P(("seq", "chan"), None))
    return jax.shard_map(
        functools.partial(local, mesh.shape["seq"]),
        mesh=mesh, in_specs=in_specs, out_specs=out_specs, check_vma=False,
    )
```

```python
import functools

import jax
import jax.numpy as jnp
import ml_dtypes
import numpy as np
from jax import lax
from jax.experimental import pallas as pl
from jax.experimental.pallas import tpu as pltpu
from jax.sharding import PartitionSpec as P

MESH = pl.DeviceIdType.MESH
F32 = jnp.float32
BF16 = jnp.bfloat16

D = 4096
MODES = 16
CB = 32
EPSILON = 1e-06
BIG = 1e30

R = 256
W = 512
H = 16
N = 8

SPLIT = 144
BATCHES = (
    ((144, 16, (0, 1, 2)), (160, 16, (1, 2, 0)), (176, 16, (2, 0, 1))),
    ((192, 32, (0, 1, 2)), (224, 16, (1, 2, 0)), (240, 16, (2, 0, 1))),
    ((0, 16, (0, 1, 2)), (16, 32, (1, 2, 0)), (48, 32, (2, 0, 1))),
    ((80, 32, (0, 1, 2)), (112, 16, (1, 2, 0)), (128, 16, (2, 0, 1))),
)
PIECES = sum(BATCHES, ())


def fourier(period, rows_in, out_from, rows_out):
    half = period // 2
    k = np.arange(half)[:, None]
    t = np.arange(rows_in)[None, :]
    angle = 2.0 * np.pi * ((k * t) % period) / period
    real, imag = np.cos(angle), -np.sin(angle)
    imag[0] = np.where(np.arange(rows_in) % 2 == 0, 1.0, -1.0)
    forward = np.concatenate([real, imag], axis=0)
    t = (out_from + np.arange(rows_out))[:, None]
    k = np.arange(half)[None, :]
    angle = 2.0 * np.pi * ((k * t) % period) / period
    real, imag = 2.0 * np.cos(angle), -2.0 * np.sin(angle)
    real[:, 0] = 1.0
    imag[:, 0] = np.where((out_from + np.arange(rows_out)) % 2 == 0, 1.0, -1.0)
    inverse = np.concatenate([real, imag], axis=1) / period
    return forward, inverse


def bits(slot):
    return (slot >> 2) & 1, (slot >> 1) & 1, slot & 1


def picked(**fixed):
    index = [slice(None)] * 3
    for name, value in fixed.items():
        index[2 - int(name[1])] = value
    return tuple(index)


def flipped(chan, slot):
    b2, b1, b0 = bits(slot)
    z, x = chan // 2, chan % 2
    if b0:
        x = 1 - x
    if b1:
        z = z + 1 - 2 * (z % 2)
    if b2:
        z = 3 - z
    return 2 * z + x


def kernel(
    n_seq,
    res_in, q_in, k_in, v_in, mix_in, liw_in, filter_in, f256_in, g256_in, f512_in, g512_in, rate_in, residue_in,
    mr_short_in, li_short_in, gain_in, slots_in,
    li_out, res_out, dec_out,
    qkv, mu, qs, ht, gated, mw, part, rb1, rb2, rb3, res_v, hb, gains, inv_gains,
    lw, lp, ql, ub, table, back, kern, lt, conv, st, sb, sr, choose, lo_v, ro_v,
    mr_filter, f256, g256, f512, g512, rate, residue, mr_short, li_short, gain, slots,
    load_sem, halo_s, halo_r, rs_s, rs_r, ag_s, ag_r, gain_s, gain_r, st_s, st_r, out_sem,
):
    seq, chan = lax.axis_index("seq"), lax.axis_index("chan")
    first = seq == 0
    pending = []

    barrier = pltpu.get_barrier_semaphore()
    after = (lax.rem(seq + 1, n_seq), chan)
    chan_peers = [(seq, flipped(chan, s)) for s in range(1, N)]
    seq_peers = [(lax.rem(seq + k, n_seq), chan) for k in range(1, n_seq)]
    for peer in chan_peers + seq_peers:
        pl.semaphore_signal(barrier, inc=1, device_id=peer, device_id_type=MESH)

    loads = []

    def load(src, dst):
        copy = pltpu.make_async_copy(src, dst, load_sem.at[len(loads)])
        copy.start()
        loads.append(copy)
        return copy

    first_loads = [load(filter_in, mr_filter), load(f256_in, f256)]
    in_loads = [load(mr_short_in, mr_short)] + [
        load(ref, qkv.at[i, pl.ds(H, R), :]) for i, ref in enumerate((q_in, k_in, v_in))
    ]
    g_load = load(g256_in, g256)
    mix_loads = [
        load(mix_in.at[:, pl.ds(pl.multiple_of(flipped(chan, s) * W, W), W)], mw.at[s]) for s in range(N)
    ]

    def remote(src, dst, send_sem, recv_sem, to):
        return pltpu.make_async_remote_copy(
            src_ref=src, dst_ref=dst, send_sem=send_sem, recv_sem=recv_sem,
            device_id=to, device_id_type=MESH,
        )

    def send(*what):
        copy = remote(*what)
        copy.start()
        pending.append(copy)
        return copy

    def hand_on(*copies):
        @pl.when(seq < n_seq - 1)
        def _():
            for copy in copies:
                copy.start()

    def handed(*copies):
        @pl.when(seq > 0)
        def _():
            for copy in copies:
                copy.wait_recv()

    def handed_on(*copies):
        @pl.when(seq < n_seq - 1)
        def _():
            for copy in copies:
                copy.wait_send()

    for copy in first_loads:
        copy.wait()
    spectrum = jnp.dot(f256[:, :128], mr_filter[...], preferred_element_type=F32)
    row = lax.broadcasted_iota(jnp.int32, (128, W), 0)
    ht[0] = spectrum[:128]
    ht[1] = jnp.where(row == 0, 0.0, spectrum[128:])
    ht[2] = jnp.where(row == 0, spectrum[128:], spectrum[:128])

    gain_load = load(gain_in, gain)
    mode_loads = [load(rate_in, rate), load(residue_in, residue)]

    def short(ext, taps, rows):
        once = pltpu.roll(ext, 1, 0)
        twice = pltpu.roll(ext, 2, 0)
        top = ext.shape[0] - rows
        return taps[0:1] * ext[top:] + taps[1:2] * once[top:] + taps[2:3] * twice[top:]

    for copy in in_loads:
        copy.wait()
    mr_taps = [mr_short[i].astype(F32) for i in range(3)]
    for c in range(W // 128):
        lanes = slice(c * 128, (c + 1) * 128)
        three = [short(qkv[i, H:, lanes].astype(F32), mr_taps[i][:, lanes], R) for i in range(3)]
        qs[:, lanes] = three[0]
        mu[128:, lanes] = (three[1] * three[2]).astype(BF16)

    def filtered(r0):
        x = jnp.dot(f256[...], mu[r0 : r0 + 256, :], preferred_element_type=F32)
        xr, xi = x[:128], x[128:]
        y = jnp.concatenate(
            [
                (xr * ht[0] - xi * ht[1]).astype(BF16),
                (xr * ht[1] + xi * ht[2]).astype(BF16),
            ],
            axis=0,
        )
        return jnp.dot(g256[...], y, preferred_element_type=F32)

    def mixed(r0, r1):
        for s in range(N):
            part[bits(s) + (slice(r0, r1), slice(None))] = jnp.dot(
                gated[r0:r1, :], mw[s], preferred_element_type=F32
            ).astype(BF16)

    def fixed_bits(g, count, last=0):
        order = PIECES[g][2]
        bit = {f"b{d}": 0 for d in order[:count]}
        if last:
            bit[f"b{order[count]}"] = 1
        return picked(**bit)

    def step_send(g, step):
        r0, n, order = PIECES[g]
        rows = (pl.ds(r0, n), slice(None))
        dim = order[(0, 1, 2, 1, 0)[step]]
        to = (seq, flipped(chan, 1 << dim))
        if step < 2:
            src = part.at[fixed_bits(g, step, 1) + rows]
            dst = rb1.at[(slice(None),) * 2 + rows] if step == 0 else rb2.at[(slice(None),) + rows]
            return send(src, dst, rs_s.at[g, step], rs_r.at[g, step], to)
        if step == 2:
            src = part.at[fixed_bits(g, 2) + rows]
            return send(src, rb3.at[(slice(None),) + rows], rs_s.at[g, 2], rs_r.at[g, 2], to)
        kept = 1 if step == 3 else 0
        src = hb.at[fixed_bits(g, kept + 1) + rows]
        dst = hb.at[fixed_bits(g, kept, 1) + rows]
        return send(src, dst, ag_s.at[g, step - 3], ag_r.at[g, step - 3], to)

    def step_work(g, step):
        r0, n, order = PIECES[g]
        rows = (slice(r0, r0 + n), slice(None))
        if step == 1:
            index = fixed_bits(g, 1) + rows
            part[index] = (part[index].astype(F32) + rb1[(slice(None),) * 2 + rows].astype(F32)).astype(BF16)
        if step in (2, 3):
            near = (0, 0, 0) + rows
            far = bits(1 << order[2]) + rows
        if step == 2:
            part[near] = (
                part[near].astype(F32) + rb2[(0,) + rows].astype(F32) + res_v[rows].astype(F32)
            ).astype(BF16)
            part[far] = (part[far].astype(F32) + rb2[(1,) + rows].astype(F32)).astype(BF16)
        if step == 3:
            total = part[near].astype(F32) + rb3[(1,) + rows].astype(F32)
            ro_v[rows] = total.astype(BF16)
            hb[near] = jnp.clip(total * gains[0], -BIG, BIG).astype(BF16)
            total = part[far].astype(F32) + rb3[(0,) + rows].astype(F32)
            hb[far] = jnp.clip(total * gains[1 << order[2]], -BIG, BIG).astype(BF16)

    flying = {}

    def advance(b, step):
        for g in range(3 * b, 3 * b + 3):
            if step > 0:
                flying[g, step - 1].wait_recv()
                step_work(g, step)
            flying[g, step] = step_send(g, step)

    def row_scale(r0, r1):
        squares = jnp.zeros((r1 - r0, 128), F32)
        for s in range(N):
            sums = hb[bits(s) + (slice(r0, r1), slice(None))].astype(F32) * inv_gains[s]
            sums = sums * sums
            for c in range(W // 128):
                squares = squares + sums[:, c * 128 : (c + 1) * 128]
        return lax.rsqrt(jnp.sum(squares, axis=1, keepdims=True) / D + EPSILON)

    def project(r0, r1, inverse, which):
        lhs = jnp.concatenate([hb[bits(s) + (slice(r0, r1), slice(None))] for s in range(N)], axis=1)
        for i in which:
            out = jnp.dot(lhs, lw[i], preferred_element_type=F32) * inverse
            lp[i, H + r0 : H + r1, :] = out.astype(BF16)

    kern[...] = jnp.zeros((R, W), F32)
    time = lax.broadcasted_iota(jnp.int32, (R, W), 0).astype(F32)

    def modes(first_mode, count):
        def mode(m, carry):
            powers = jnp.exp(-rate[pl.ds(m, 1), :] * time)
            table[m] = powers
            kern[...] += residue[pl.ds(m, 1), :] * powers
            back[m] = jnp.exp(-rate[pl.ds(m, 1), :] * (R - 1.0 - time))
            return carry

        lax.fori_loop(first_mode, first_mode + count, mode, 0)

    def kernel_spectrum():
        spectrum = jnp.dot(f512[...], kern[...].astype(BF16), preferred_element_type=F32)
        row = lax.broadcasted_iota(jnp.int32, (256, W), 0)
        lt[0] = spectrum[:256]
        lt[1] = jnp.where(row == 0, 0.0, spectrum[256:])
        lt[2] = jnp.where(row == 0, spectrum[256:], spectrum[:256])

    li_taps = []

    def li_short_rows(i, r0, r1, lanes):
        ext = lp[i, r0 : H + r1, lanes].astype(F32)
        if r0 == 0:
            ext_row = lax.broadcasted_iota(jnp.int32, ext.shape, 0)
            ext = jnp.where(jnp.logical_and(first, ext_row < H), 0.0, ext)
        return short(ext, li_taps[i][:, lanes], r1 - r0)

    def li_queries(r0, r1):
        for c in range(W // 128):
            lanes = slice(c * 128, (c + 1) * 128)
            ql[r0:r1, lanes] = li_short_rows(0, r0, r1, lanes)

    def li_inputs(r0, r1):
        for c in range(W // 128):
            lanes = slice(c * 128, (c + 1) * 128)
            product = li_short_rows(1, r0, r1, lanes) * li_short_rows(2, r0, r1, lanes)
            ub[r0:r1, lanes] = product.astype(BF16)
        values = ub[r0:r1, :].astype(F32)

        def ends(j, carry):
            for i in range(4):
                m = 4 * j + i
                st[pl.ds(m, 1), :] += jnp.sum(back[m, r0:r1, :] * values, axis=0, keepdims=True)
            return carry

        lax.fori_loop(0, MODES // 4, ends, 0)

    g_load.wait()
    out = filtered(128)
    gated[SPLIT:, :] = (qs[SPLIT:, :] * out[SPLIT - 128 :]).astype(BF16)
    for copy in mix_loads:
        copy.wait()
    mixed(SPLIT, 192)
    pl.semaphore_wait(barrier, N - 1 + n_seq - 1)
    halos = [
        remote(qkv.at[i, pl.ds(R, H), :], qkv.at[i, pl.ds(0, H), :], halo_s.at[i], halo_r.at[i], after)
        for i in range(3)
    ]
    rim = remote(mu.at[pl.ds(R, 128), :], mu.at[pl.ds(0, 128), :], halo_s.at[3], halo_r.at[3], after)
    hand_on(*halos, rim)
    advance(0, 0)
    mixed(192, R)
    advance(1, 0)

    gain_load.wait()
    gains[0] = gain[...].astype(F32).reshape(1, W)
    gain_sends = [
        send(gains.at[0], gains.at[s], gain_s.at[s - 1], gain_r.at[s - 1], chan_peers[s - 1])
        for s in range(1, N)
    ]
    res_load = load(res_in, res_v)
    more_loads = [load(f512_in, f512), load(g512_in, g512), load(li_short_in, li_short), load(slots_in, slots)]
    li_loads = [
        load(liw_in.at[:, pl.ds(pl.multiple_of(flipped(chan, s) * W, W), W), :], lw.at[:, pl.ds(s * W, W), :])
        for s in range(N)
    ]
    for copy in mode_loads:
        copy.wait()
    modes(0, 4)

    advance(0, 1)

    handed(*halos)
    fixed = []
    ext_row = lax.broadcasted_iota(jnp.int32, (2 * H, W), 0)
    outside = jnp.logical_and(first, ext_row < H)
    for i in range(3):
        ext = jnp.where(outside, 0.0, qkv[i, : 2 * H, :].astype(F32))
        fixed.append(short(ext, mr_taps[i], H))
    qs[:H, :] = fixed[0]
    right = (fixed[1] * fixed[2]).astype(BF16)
    missed = (right.astype(F32) - mu[128 : 128 + H, :].astype(F32))[1:2] * mr_filter[127:128, :].astype(F32)
    mu[128 : 128 + H, :] = right
    ahead = out[: SPLIT - 128]
    ahead = ahead + jnp.where(lax.broadcasted_iota(jnp.int32, ahead.shape, 0) == 0, missed, 0.0)
    gated[128:SPLIT, :] = (qs[128:SPLIT, :] * ahead).astype(BF16)
    handed(rim)
    mu[:128, :] = jnp.where(first, jnp.zeros((128, W), BF16), mu[:128, :])
    gated[:128, :] = (qs[:128, :] * filtered(0)).astype(BF16)
    mixed(0, 80)
    advance(2, 0)
    mixed(80, SPLIT)
    advance(3, 0)

    advance(1, 1)
    modes(4, 4)
    res_load.wait()
    for copy in gain_sends:
        copy.wait_recv()
    for s in range(N):
        inv_gains[s] = 1.0 / gains[s]
    advance(0, 2)
    modes(8, 4)
    advance(2, 1)
    advance(3, 1)
    advance(1, 2)
    advance(0, 3)
    modes(12, 4)
    advance(2, 2)
    advance(3, 2)
    advance(1, 3)
    advance(0, 4)
    for copy in more_loads:
        copy.wait()
    advance(2, 3)
    advance(3, 3)
    advance(1, 4)
    res_store = pltpu.make_async_copy(ro_v, res_out, out_sem.at[0])
    res_store.start()
    for copy in li_loads:
        copy.wait()
    li_taps.extend(li_short[i].astype(F32) for i in range(3))
    st[...] = jnp.zeros((MODES, W), F32)
    advance(2, 4)
    advance(3, 4)

    def arrived(*batches):
        for b in batches:
            for g in range(3 * b, 3 * b + 3):
                flying[g, 4].wait_recv()

    arrived(0, 1)
    inverse = row_scale(SPLIT, R)
    last, border = pl.ds(R, H), pl.ds(0, H)
    both = pl.ds(1, 2)
    li_halo = remote(lp.at[both, last, :], lp.at[both, border, :], halo_s.at[4], halo_r.at[4], after)
    query_halo = remote(lp.at[0, last, :], lp.at[0, border, :], halo_s.at[5], halo_r.at[5], after)
    project(SPLIT, R, inverse, (1, 2))
    hand_on(li_halo)
    li_inputs(160, R)
    project(SPLIT, R, inverse, (0,))
    hand_on(query_halo)
    arrived(2, 3)
    inverse = row_scale(0, SPLIT)
    project(0, SPLIT, inverse, (1, 2))
    handed(li_halo)
    li_inputs(0, 160)
    sb[...] = st[...].astype(BF16)
    states = [send(sb, sr.at[k + 1], st_s.at[k], st_r.at[k], seq_peers[k]) for k in range(n_seq - 1)]
    project(0, SPLIT, inverse, (0,))
    li_queries(160, R)
    handed(query_halo)
    li_queries(0, 160)

    kernel_spectrum()
    x = jnp.dot(f512[...], ub[...], preferred_element_type=F32)
    xr, xi = x[:256], x[256:]
    y = jnp.concatenate(
        [
            (xr * lt[0] - xi * lt[1]).astype(BF16),
            (xr * lt[1] + xi * lt[2]).astype(BF16),
        ],
        axis=0,
    )
    conv[...] = jnp.dot(g512[...], y, preferred_element_type=F32)

    mine = seq * N + chan
    block = jnp.int32(0)
    for b in range(slots.shape[0]):
        block = block + jnp.where(slots[b] == mine, jnp.int32(b), jnp.int32(0))
    source = lax.broadcasted_iota(jnp.int32, (W, W), 0) - block * CB
    target = lax.broadcasted_iota(jnp.int32, (W, W), 1) // MODES
    choose[...] = jnp.where(source == target, 1.0, 0.0).astype(BF16)

    sr[0] = sb[...]
    decay = jnp.exp(-rate[...] * float(R))
    leaving = residue[...] * jnp.exp(-rate[...])
    for copy in states:
        copy.wait_recv()
    incoming = jnp.zeros((MODES, W), F32)
    for k in range(n_seq - 1, 0, -1):
        incoming = incoming * decay + jnp.where(seq >= k, sr[k].astype(F32), 0.0)
    st[...] = incoming * leaving

    def across(j, carry):
        rows = pl.ds(pl.multiple_of(j * 32, 32), 32)
        total = conv[rows, :]
        for m in range(MODES):
            total = total + st[m : m + 1, :] * table[m, rows, :]
        lo_v[rows, :] = (ql[rows, :] * total).astype(BF16)
        return carry

    stores = [res_store]
    for i in range(2):
        lax.fori_loop(i * R // 64, (i + 1) * R // 64, across, 0)
        rows = pl.ds(i * (R // 2), R // 2)
        stores.append(pltpu.make_async_copy(lo_v.at[rows, :], li_out.at[rows, :], out_sem.at[1 + i]))
        stores[-1].start()

    final = jnp.zeros((MODES, W), F32)
    for j in range(n_seq):
        final = final * decay + sr[lax.rem(seq + n_seq - j, n_seq)].astype(F32)
    final = final * residue[...]
    high = final.astype(BF16)
    low = (final - high.astype(F32)).astype(BF16)
    chosen = jnp.dot(high, choose[...], preferred_element_type=F32) + jnp.dot(
        low, choose[...], preferred_element_type=F32
    )
    m_row = lax.broadcasted_iota(jnp.int32, (MODES, W), 0)
    m_lane = lax.broadcasted_iota(jnp.int32, (MODES, W), 1) % MODES
    dec_out[...] = jnp.sum(jnp.where(m_row == m_lane, chosen, 0.0), axis=0, keepdims=True)

    handed_on(*halos, rim, li_halo, query_halo)
    for copy in pending:
        copy.wait_send()
    for copy in stores:
        copy.wait()


def hand_over(li_in, res_in, dec_in, li_out, res_out, dec_out, li_v, res_v, dec_v, sem):
    trips = ((li_in, li_v, li_out), (res_in, res_v, res_out), (dec_in, dec_v, dec_out))
    there = [pltpu.make_async_copy(src, held, sem.at[0, i]) for i, (src, held, _) in enumerate(trips)]
    again = [pltpu.make_async_copy(held, dst, sem.at[1, i]) for i, (_, held, dst) in enumerate(trips)]
    for copy in there:
        copy.start()
    for copy, later in zip(there, again):
        copy.wait()
        later.start()
    for copy in again:
        copy.wait()


def local(n_seq, residual_in, mr_query, mr_key, mr_value, mr_short, mr_filter, mix_weight, norm_gain,
          li_weight, li_short, li_rate, li_residue, decode_slot):
    f256, g256 = fourier(256, 256, 128, 128)
    f512, g512 = fourier(512, 256, 0, 256)
    tables = [jnp.asarray(a.astype(np.float32).astype(ml_dtypes.bfloat16)) for a in (f256, g256, f512, g512)]
    hbm = pl.BlockSpec(memory_space=pltpu.HBM)
    vmem = pl.BlockSpec(memory_space=pltpu.VMEM)
    v = pltpu.VMEM
    dma = pltpu.SemaphoreType.DMA
    shapes = (
        jax.ShapeDtypeStruct((R, W), BF16),
        jax.ShapeDtypeStruct((R, W), BF16),
        jax.ShapeDtypeStruct((1, CB * MODES), F32),
    )
    done = pl.pallas_call(
        functools.partial(kernel, n_seq),
        out_shape=shapes,
        in_specs=[hbm] * 17,
        out_specs=(hbm, hbm, vmem),
        scratch_shapes=[
            v((3, H + R, W), BF16),
            v((128 + R, W), BF16),
            v((R, W), F32),
            v((3, 128, W), F32),
            v((R, W), BF16),
            v((N, W, W), BF16),
            v((2, 2, 2, R, W), BF16),
            v((2, 2, R, W), BF16),
            v((2, R, W), BF16),
            v((2, R, W), BF16),
            v((R, W), BF16),
            v((2, 2, 2, R, W), BF16),
            v((N, 1, W), F32),
            v((N, 1, W), F32),
            v((3, N * W, W), BF16),
            v((3, H + R, W), BF16),
            v((R, W), F32),
            v((R, W), BF16),
            v((MODES, R, W), F32),
            v((MODES, R, W), F32),
            v((R, W), F32),
            v((3, 256, W), F32),
            v((R, W), F32),
            v((MODES, W), F32),
            v((MODES, W), BF16),
            v((n_seq, MODES, W), BF16),
            v((W, W), BF16),
            v((R, W), BF16),
            v((R, W), BF16),
            v((128, W), BF16),
            v((256, 256), BF16),
            v((128, 256), BF16),
            v((512, 256), BF16),
            v((256, 512), BF16),
            v((MODES, W), F32),
            v((MODES, W), F32),
            v((3, 3, W), BF16),
            v((3, 3, W), BF16),
            v((W,), BF16),
            pltpu.SMEM((16,), jnp.int32),
            dma((31,)),
            dma((6,)), dma((6,)),
            dma((len(PIECES), 3)), dma((len(PIECES), 3)),
            dma((len(PIECES), 2)), dma((len(PIECES), 2)),
            dma((N - 1,)), dma((N - 1,)),
            dma((n_seq - 1,)), dma((n_seq - 1,)),
            dma((3,)),
        ],
        compiler_params=pltpu.CompilerParams(
            collective_id=0, has_side_effects=True, vmem_limit_bytes=60 * 1024 * 1024
        ),
        name="layers",
    )(
        residual_in, mr_query, mr_key, mr_value, mix_weight, li_weight, mr_filter, *tables, li_rate.T, li_residue.T,
        mr_short, li_short, norm_gain, decode_slot,
    )
    return pl.pallas_call(
        hand_over,
        out_shape=shapes,
        in_specs=[hbm] * 3,
        out_specs=(hbm,) * 3,
        scratch_shapes=[v((R, W), BF16), v((R, W), BF16), v((1, CB * MODES), F32), dma((2, 3))],
        compiler_params=pltpu.CompilerParams(vmem_limit_bytes=60 * 1024 * 1024),
        name="hand_over",
    )(*done)


def solution(mesh):
    in_specs = (
        P("seq", "chan"), P("seq", "chan"), P("seq", "chan"), P("seq", "chan"),
        P(None, None, "chan"), P(None, "chan"), P("chan", None), P("chan"),
        P(None, None, "chan"), P(None, None, "chan"), P("chan", None), P("chan", None), P("chan"),
    )
    out_specs = (P("seq", "chan"), P("seq", "chan"), P(("seq", "chan"), None))
    return jax.shard_map(
        functools.partial(local, mesh.shape["seq"]),
        mesh=mesh, in_specs=in_specs, out_specs=out_specs, check_vma=False,
    )
```

```python
import functools

import jax
import jax.numpy as jnp
import ml_dtypes
import numpy as np
from jax import lax
from jax.experimental import pallas as pl
from jax.experimental.pallas import tpu as pltpu
from jax.sharding import PartitionSpec as P

MESH = pl.DeviceIdType.MESH
F32 = jnp.float32
BF16 = jnp.bfloat16

D = 4096
MODES = 16
CB = 32
EPSILON = 1e-06
BIG = 1e30

R = 256
W = 512
H = 16
N = 8

SPLIT = 144
BATCHES = (
    ((144, 16, (0, 1, 2)), (160, 16, (1, 2, 0)), (176, 16, (2, 0, 1))),
    ((192, 32, (0, 1, 2)), (224, 16, (1, 2, 0)), (240, 16, (2, 0, 1))),
    ((0, 16, (0, 1, 2)), (16, 32, (1, 2, 0)), (48, 32, (2, 0, 1))),
    ((80, 32, (0, 1, 2)), (112, 16, (1, 2, 0)), (128, 16, (2, 0, 1))),
)
PIECES = sum(BATCHES, ())


def fourier(period, rows_in, out_from, rows_out):
    half = period // 2
    k = np.arange(half)[:, None]
    t = np.arange(rows_in)[None, :]
    angle = 2.0 * np.pi * ((k * t) % period) / period
    real, imag = np.cos(angle), -np.sin(angle)
    imag[0] = np.where(np.arange(rows_in) % 2 == 0, 1.0, -1.0)
    forward = np.concatenate([real, imag], axis=0)
    t = (out_from + np.arange(rows_out))[:, None]
    k = np.arange(half)[None, :]
    angle = 2.0 * np.pi * ((k * t) % period) / period
    real, imag = 2.0 * np.cos(angle), -2.0 * np.sin(angle)
    real[:, 0] = 1.0
    imag[:, 0] = np.where((out_from + np.arange(rows_out)) % 2 == 0, 1.0, -1.0)
    inverse = np.concatenate([real, imag], axis=1) / period
    return forward, inverse


def bits(slot):
    return (slot >> 2) & 1, (slot >> 1) & 1, slot & 1


def picked(**fixed):
    index = [slice(None)] * 3
    for name, value in fixed.items():
        index[2 - int(name[1])] = value
    return tuple(index)


def flipped(chan, slot):
    b2, b1, b0 = bits(slot)
    z, x = chan // 2, chan % 2
    if b0:
        x = 1 - x
    if b1:
        z = z + 1 - 2 * (z % 2)
    if b2:
        z = 3 - z
    return 2 * z + x


def kernel(
    n_seq,
    res_in, q_in, k_in, v_in, mix_in, liw_in, filter_in, f256_in, g256_in, f512_in, g512_in, rate_in, residue_in,
    mr_short_in, li_short_in, gain_in, slots_in,
    li_out, res_out, dec_out,
    qkv, mu, qs, ht, gated, mw, part, rb1, rb2, rb3, res_v, hb, gains, inv_gains,
    lw, lp, ql, ub, table, back, kern, lt, conv, st, sb, sr, choose, lo_v, ro_v, dec_v,
    mr_filter, f256, g256, f512, g512, rate, residue, mr_short, li_short, gain, slots,
    load_sem, halo_s, halo_r, rs_s, rs_r, ag_s, ag_r, gain_s, gain_r, st_s, st_r, out_sem,
):
    seq, chan = lax.axis_index("seq"), lax.axis_index("chan")
    first = seq == 0
    pending = []

    barrier = pltpu.get_barrier_semaphore()
    after = (lax.rem(seq + 1, n_seq), chan)
    chan_peers = [(seq, flipped(chan, s)) for s in range(1, N)]
    seq_peers = [(lax.rem(seq + k, n_seq), chan) for k in range(1, n_seq)]
    for peer in chan_peers + seq_peers:
        pl.semaphore_signal(barrier, inc=1, device_id=peer, device_id_type=MESH)

    loads = []

    def load(src, dst):
        copy = pltpu.make_async_copy(src, dst, load_sem.at[len(loads)])
        copy.start()
        loads.append(copy)
        return copy

    first_loads = [load(filter_in, mr_filter), load(f256_in, f256)]
    in_loads = [load(mr_short_in, mr_short)] + [
        load(ref, qkv.at[i, pl.ds(H, R), :]) for i, ref in enumerate((q_in, k_in, v_in))
    ]
    g_load = load(g256_in, g256)
    mix_loads = [
        load(mix_in.at[:, pl.ds(pl.multiple_of(flipped(chan, s) * W, W), W)], mw.at[s]) for s in range(N)
    ]

    def remote(src, dst, send_sem, recv_sem, to):
        return pltpu.make_async_remote_copy(
            src_ref=src, dst_ref=dst, send_sem=send_sem, recv_sem=recv_sem,
            device_id=to, device_id_type=MESH,
        )

    def send(*what):
        copy = remote(*what)
        copy.start()
        pending.append(copy)
        return copy

    def hand_on(*copies):
        @pl.when(seq < n_seq - 1)
        def _():
            for copy in copies:
                copy.start()

    def handed(*copies):
        @pl.when(seq > 0)
        def _():
            for copy in copies:
                copy.wait_recv()

    def handed_on(*copies):
        @pl.when(seq < n_seq - 1)
        def _():
            for copy in copies:
                copy.wait_send()

    for copy in first_loads:
        copy.wait()
    spectrum = jnp.dot(f256[:, :128], mr_filter[...], preferred_element_type=F32)
    row = lax.broadcasted_iota(jnp.int32, (128, W), 0)
    ht[0] = spectrum[:128]
    ht[1] = jnp.where(row == 0, 0.0, spectrum[128:])
    ht[2] = jnp.where(row == 0, spectrum[128:], spectrum[:128])

    gain_load = load(gain_in, gain)
    mode_loads = [load(rate_in, rate), load(residue_in, residue)]

    def short(ext, taps, rows):
        once = pltpu.roll(ext, 1, 0)
        twice = pltpu.roll(ext, 2, 0)
        top = ext.shape[0] - rows
        return taps[0:1] * ext[top:] + taps[1:2] * once[top:] + taps[2:3] * twice[top:]

    for copy in in_loads:
        copy.wait()
    mr_taps = [mr_short[i].astype(F32) for i in range(3)]
    for c in range(W // 128):
        lanes = slice(c * 128, (c + 1) * 128)
        three = [short(qkv[i, H:, lanes].astype(F32), mr_taps[i][:, lanes], R) for i in range(3)]
        qs[:, lanes] = three[0]
        mu[128:, lanes] = (three[1] * three[2]).astype(BF16)

    def filtered(r0):
        x = jnp.dot(f256[...], mu[r0 : r0 + 256, :], preferred_element_type=F32)
        xr, xi = x[:128], x[128:]
        y = jnp.concatenate(
            [
                (xr * ht[0] - xi * ht[1]).astype(BF16),
                (xr * ht[1] + xi * ht[2]).astype(BF16),
            ],
            axis=0,
        )
        return jnp.dot(g256[...], y, preferred_element_type=F32)

    def mixed(r0, r1):
        for s in range(N):
            part[bits(s) + (slice(r0, r1), slice(None))] = jnp.dot(
                gated[r0:r1, :], mw[s], preferred_element_type=F32
            ).astype(BF16)

    def fixed_bits(g, count, last=0):
        order = PIECES[g][2]
        bit = {f"b{d}": 0 for d in order[:count]}
        if last:
            bit[f"b{order[count]}"] = 1
        return picked(**bit)

    def step_send(g, step):
        r0, n, order = PIECES[g]
        rows = (pl.ds(r0, n), slice(None))
        dim = order[(0, 1, 2, 1, 0)[step]]
        to = (seq, flipped(chan, 1 << dim))
        if step < 2:
            src = part.at[fixed_bits(g, step, 1) + rows]
            dst = rb1.at[(slice(None),) * 2 + rows] if step == 0 else rb2.at[(slice(None),) + rows]
            return send(src, dst, rs_s.at[g, step], rs_r.at[g, step], to)
        if step == 2:
            src = part.at[fixed_bits(g, 2) + rows]
            return send(src, rb3.at[(slice(None),) + rows], rs_s.at[g, 2], rs_r.at[g, 2], to)
        kept = 1 if step == 3 else 0
        src = hb.at[fixed_bits(g, kept + 1) + rows]
        dst = hb.at[fixed_bits(g, kept, 1) + rows]
        return send(src, dst, ag_s.at[g, step - 3], ag_r.at[g, step - 3], to)

    def step_work(g, step):
        r0, n, order = PIECES[g]
        rows = (slice(r0, r0 + n), slice(None))
        if step == 1:
            index = fixed_bits(g, 1) + rows
            part[index] = (part[index].astype(F32) + rb1[(slice(None),) * 2 + rows].astype(F32)).astype(BF16)
        if step in (2, 3):
            near = (0, 0, 0) + rows
            far = bits(1 << order[2]) + rows
        if step == 2:
            part[near] = (
                part[near].astype(F32) + rb2[(0,) + rows].astype(F32) + res_v[rows].astype(F32)
            ).astype(BF16)
            part[far] = (part[far].astype(F32) + rb2[(1,) + rows].astype(F32)).astype(BF16)
        if step == 3:
            total = part[near].astype(F32) + rb3[(1,) + rows].astype(F32)
            ro_v[rows] = total.astype(BF16)
            hb[near] = jnp.clip(total * gains[0], -BIG, BIG).astype(BF16)
            total = part[far].astype(F32) + rb3[(0,) + rows].astype(F32)
            hb[far] = jnp.clip(total * gains[1 << order[2]], -BIG, BIG).astype(BF16)

    flying = {}

    def advance(b, step):
        for g in range(3 * b, 3 * b + 3):
            if step > 0:
                flying[g, step - 1].wait_recv()
                step_work(g, step)
            flying[g, step] = step_send(g, step)

    def row_scale(r0, r1):
        squares = jnp.zeros((r1 - r0, 128), F32)
        for s in range(N):
            sums = hb[bits(s) + (slice(r0, r1), slice(None))].astype(F32) * inv_gains[s]
            sums = sums * sums
            for c in range(W // 128):
                squares = squares + sums[:, c * 128 : (c + 1) * 128]
        return lax.rsqrt(jnp.sum(squares, axis=1, keepdims=True) / D + EPSILON)

    def project(r0, r1, inverse, which):
        lhs = jnp.concatenate([hb[bits(s) + (slice(r0, r1), slice(None))] for s in range(N)], axis=1)
        for i in which:
            out = jnp.dot(lhs, lw[i], preferred_element_type=F32) * inverse
            lp[i, H + r0 : H + r1, :] = out.astype(BF16)

    kern[...] = jnp.zeros((R, W), F32)
    time = lax.broadcasted_iota(jnp.int32, (R, W), 0).astype(F32)

    def modes(first_mode, count):
        def mode(m, carry):
            powers = jnp.exp(-rate[pl.ds(m, 1), :] * time)
            table[m] = powers
            kern[...] += residue[pl.ds(m, 1), :] * powers
            back[m] = jnp.exp(-rate[pl.ds(m, 1), :] * (R - 1.0 - time))
            return carry

        lax.fori_loop(first_mode, first_mode + count, mode, 0)

    def kernel_spectrum():
        spectrum = jnp.dot(f512[...], kern[...].astype(BF16), preferred_element_type=F32)
        row = lax.broadcasted_iota(jnp.int32, (256, W), 0)
        lt[0] = spectrum[:256]
        lt[1] = jnp.where(row == 0, 0.0, spectrum[256:])
        lt[2] = jnp.where(row == 0, spectrum[256:], spectrum[:256])

    li_taps = []

    def li_short_rows(i, r0, r1, lanes):
        ext = lp[i, r0 : H + r1, lanes].astype(F32)
        if r0 == 0:
            ext_row = lax.broadcasted_iota(jnp.int32, ext.shape, 0)
            ext = jnp.where(jnp.logical_and(first, ext_row < H), 0.0, ext)
        return short(ext, li_taps[i][:, lanes], r1 - r0)

    def li_queries(r0, r1):
        for c in range(W // 128):
            lanes = slice(c * 128, (c + 1) * 128)
            ql[r0:r1, lanes] = li_short_rows(0, r0, r1, lanes)

    def li_inputs(r0, r1):
        for c in range(W // 128):
            lanes = slice(c * 128, (c + 1) * 128)
            product = li_short_rows(1, r0, r1, lanes) * li_short_rows(2, r0, r1, lanes)
            ub[r0:r1, lanes] = product.astype(BF16)
        values = ub[r0:r1, :].astype(F32)

        def ends(j, carry):
            for i in range(4):
                m = 4 * j + i
                st[pl.ds(m, 1), :] += jnp.sum(back[m, r0:r1, :] * values, axis=0, keepdims=True)
            return carry

        lax.fori_loop(0, MODES // 4, ends, 0)

    g_load.wait()
    out = filtered(128)
    gated[SPLIT:, :] = (qs[SPLIT:, :] * out[SPLIT - 128 :]).astype(BF16)
    for copy in mix_loads:
        copy.wait()
    mixed(SPLIT, 192)
    pl.semaphore_wait(barrier, N - 1 + n_seq - 1)
    halos = [
        remote(qkv.at[i, pl.ds(R, H), :], qkv.at[i, pl.ds(0, H), :], halo_s.at[i], halo_r.at[i], after)
        for i in range(3)
    ]
    rim = remote(mu.at[pl.ds(R, 128), :], mu.at[pl.ds(0, 128), :], halo_s.at[3], halo_r.at[3], after)
    hand_on(*halos, rim)
    advance(0, 0)
    mixed(192, R)
    advance(1, 0)

    gain_load.wait()
    gains[0] = gain[...].astype(F32).reshape(1, W)
    gain_sends = [
        send(gains.at[0], gains.at[s], gain_s.at[s - 1], gain_r.at[s - 1], chan_peers[s - 1])
        for s in range(1, N)
    ]
    res_load = load(res_in, res_v)
    more_loads = [load(f512_in, f512), load(g512_in, g512), load(li_short_in, li_short), load(slots_in, slots)]
    li_loads = [
        load(liw_in.at[:, pl.ds(pl.multiple_of(flipped(chan, s) * W, W), W), :], lw.at[:, pl.ds(s * W, W), :])
        for s in range(N)
    ]
    for copy in mode_loads:
        copy.wait()
    modes(0, 4)

    advance(0, 1)

    handed(*halos)
    fixed = []
    ext_row = lax.broadcasted_iota(jnp.int32, (2 * H, W), 0)
    outside = jnp.logical_and(first, ext_row < H)
    for i in range(3):
        ext = jnp.where(outside, 0.0, qkv[i, : 2 * H, :].astype(F32))
        fixed.append(short(ext, mr_taps[i], H))
    qs[:H, :] = fixed[0]
    right = (fixed[1] * fixed[2]).astype(BF16)
    missed = (right.astype(F32) - mu[128 : 128 + H, :].astype(F32))[1:2] * mr_filter[127:128, :].astype(F32)
    mu[128 : 128 + H, :] = right
    ahead = out[: SPLIT - 128]
    ahead = ahead + jnp.where(lax.broadcasted_iota(jnp.int32, ahead.shape, 0) == 0, missed, 0.0)
    gated[128:SPLIT, :] = (qs[128:SPLIT, :] * ahead).astype(BF16)
    handed(rim)
    mu[:128, :] = jnp.where(first, jnp.zeros((128, W), BF16), mu[:128, :])
    gated[:128, :] = (qs[:128, :] * filtered(0)).astype(BF16)
    mixed(0, 80)
    advance(2, 0)
    mixed(80, SPLIT)
    advance(3, 0)

    advance(1, 1)
    modes(4, 4)
    res_load.wait()
    for copy in gain_sends:
        copy.wait_recv()
    for s in range(N):
        inv_gains[s] = 1.0 / gains[s]
    advance(0, 2)
    modes(8, 4)
    advance(2, 1)
    advance(3, 1)
    advance(1, 2)
    advance(0, 3)
    modes(12, 4)
    advance(2, 2)
    advance(3, 2)
    advance(1, 3)
    advance(0, 4)
    for copy in more_loads:
        copy.wait()
    advance(2, 3)
    advance(3, 3)
    advance(1, 4)
    res_store = pltpu.make_async_copy(ro_v, res_out, out_sem.at[0])
    res_store.start()
    for copy in li_loads:
        copy.wait()
    li_taps.extend(li_short[i].astype(F32) for i in range(3))
    st[...] = jnp.zeros((MODES, W), F32)
    advance(2, 4)
    advance(3, 4)

    def arrived(*batches):
        for b in batches:
            for g in range(3 * b, 3 * b + 3):
                flying[g, 4].wait_recv()

    arrived(0, 1)
    inverse = row_scale(SPLIT, R)
    last, border = pl.ds(R, H), pl.ds(0, H)
    both = pl.ds(1, 2)
    li_halo = remote(lp.at[both, last, :], lp.at[both, border, :], halo_s.at[4], halo_r.at[4], after)
    query_halo = remote(lp.at[0, last, :], lp.at[0, border, :], halo_s.at[5], halo_r.at[5], after)
    project(SPLIT, R, inverse, (1, 2))
    hand_on(li_halo)
    li_inputs(160, R)
    project(SPLIT, R, inverse, (0,))
    hand_on(query_halo)
    arrived(2, 3)
    inverse = row_scale(0, SPLIT)
    project(0, SPLIT, inverse, (1, 2))
    handed(li_halo)
    li_inputs(0, 160)
    sb[...] = st[...].astype(BF16)
    states = [send(sb, sr.at[k + 1], st_s.at[k], st_r.at[k], seq_peers[k]) for k in range(n_seq - 1)]
    project(0, SPLIT, inverse, (0,))
    li_queries(160, R)
    handed(query_halo)
    li_queries(0, 160)

    kernel_spectrum()
    x = jnp.dot(f512[...], ub[...], preferred_element_type=F32)
    xr, xi = x[:256], x[256:]
    y = jnp.concatenate(
        [
            (xr * lt[0] - xi * lt[1]).astype(BF16),
            (xr * lt[1] + xi * lt[2]).astype(BF16),
        ],
        axis=0,
    )
    conv[...] = jnp.dot(g512[...], y, preferred_element_type=F32)

    mine = seq * N + chan
    block = jnp.int32(0)
    for b in range(slots.shape[0]):
        block = block + jnp.where(slots[b] == mine, jnp.int32(b), jnp.int32(0))
    source = lax.broadcasted_iota(jnp.int32, (W, W), 0) - block * CB
    target = lax.broadcasted_iota(jnp.int32, (W, W), 1) // MODES
    choose[...] = jnp.where(source == target, 1.0, 0.0).astype(BF16)

    sr[0] = sb[...]
    decay = jnp.exp(-rate[...] * float(R))
    leaving = residue[...] * jnp.exp(-rate[...])
    for copy in states:
        copy.wait_recv()
    incoming = jnp.zeros((MODES, W), F32)
    for k in range(n_seq - 1, 0, -1):
        incoming = incoming * decay + jnp.where(seq >= k, sr[k].astype(F32), 0.0)
    st[...] = incoming * leaving

    def across(j, carry):
        rows = pl.ds(pl.multiple_of(j * 32, 32), 32)
        total = conv[rows, :]
        for m in range(MODES):
            total = total + st[m : m + 1, :] * table[m, rows, :]
        lo_v[rows, :] = (ql[rows, :] * total).astype(BF16)
        return carry

    stores = [res_store]
    for i in range(2):
        lax.fori_loop(i * R // 64, (i + 1) * R // 64, across, 0)
        rows = pl.ds(i * (R // 2), R // 2)
        stores.append(pltpu.make_async_copy(lo_v.at[rows, :], li_out.at[rows, :], out_sem.at[1 + i]))
        stores[-1].start()

    final = jnp.zeros((MODES, W), F32)
    for j in range(n_seq):
        final = final * decay + sr[lax.rem(seq + n_seq - j, n_seq)].astype(F32)
    final = final * residue[...]
    high = final.astype(BF16)
    low = (final - high.astype(F32)).astype(BF16)
    chosen = jnp.dot(high, choose[...], preferred_element_type=F32) + jnp.dot(
        low, choose[...], preferred_element_type=F32
    )
    m_row = lax.broadcasted_iota(jnp.int32, (MODES, W), 0)
    m_lane = lax.broadcasted_iota(jnp.int32, (MODES, W), 1) % MODES
    dec_v[...] = jnp.sum(jnp.where(m_row == m_lane, chosen, 0.0), axis=0, keepdims=True)
    stores.append(pltpu.make_async_copy(dec_v, dec_out, out_sem.at[3]))
    stores[-1].start()

    handed_on(*halos, rim, li_halo, query_halo)
    for copy in pending:
        copy.wait_send()
    for copy in stores:
        copy.wait()


def hand_over(li_in, res_in, dec_in, li_out, res_out, dec_out, li_v, res_v, dec_v, sem):
    trips = ((li_in, li_v, li_out), (res_in, res_v, res_out), (dec_in, dec_v, dec_out))
    there = [pltpu.make_async_copy(src, held, sem.at[0, i]) for i, (src, held, _) in enumerate(trips)]
    again = [pltpu.make_async_copy(held, dst, sem.at[1, i]) for i, (_, held, dst) in enumerate(trips)]
    for copy in there:
        copy.start()
    for copy, later in zip(there, again):
        copy.wait()
        later.start()
    for copy in again:
        copy.wait()


def local(n_seq, residual_in, mr_query, mr_key, mr_value, mr_short, mr_filter, mix_weight, norm_gain,
          li_weight, li_short, li_rate, li_residue, decode_slot):
    f256, g256 = fourier(256, 256, 128, 128)
    f512, g512 = fourier(512, 256, 0, 256)
    tables = [jnp.asarray(a.astype(np.float32).astype(ml_dtypes.bfloat16)) for a in (f256, g256, f512, g512)]
    hbm = pl.BlockSpec(memory_space=pltpu.HBM)
    vmem = pl.BlockSpec(memory_space=pltpu.VMEM)
    v = pltpu.VMEM
    dma = pltpu.SemaphoreType.DMA
    shapes = (
        jax.ShapeDtypeStruct((R, W), BF16),
        jax.ShapeDtypeStruct((R, W), BF16),
        jax.ShapeDtypeStruct((1, CB * MODES), F32),
    )
    done = pl.pallas_call(
        functools.partial(kernel, n_seq),
        out_shape=shapes,
        in_specs=[hbm] * 17,
        out_specs=(hbm, hbm, hbm),
        scratch_shapes=[
            v((3, H + R, W), BF16),
            v((128 + R, W), BF16),
            v((R, W), F32),
            v((3, 128, W), F32),
            v((R, W), BF16),
            v((N, W, W), BF16),
            v((2, 2, 2, R, W), BF16),
            v((2, 2, R, W), BF16),
            v((2, R, W), BF16),
            v((2, R, W), BF16),
            v((R, W), BF16),
            v((2, 2, 2, R, W), BF16),
            v((N, 1, W), F32),
            v((N, 1, W), F32),
            v((3, N * W, W), BF16),
            v((3, H + R, W), BF16),
            v((R, W), F32),
            v((R, W), BF16),
            v((MODES, R, W), F32),
            v((MODES, R, W), F32),
            v((R, W), F32),
            v((3, 256, W), F32),
            v((R, W), F32),
            v((MODES, W), F32),
            v((MODES, W), BF16),
            v((n_seq, MODES, W), BF16),
            v((W, W), BF16),
            v((R, W), BF16),
            v((R, W), BF16),
            v((1, CB * MODES), F32),
            v((128, W), BF16),
            v((256, 256), BF16),
            v((128, 256), BF16),
            v((512, 256), BF16),
            v((256, 512), BF16),
            v((MODES, W), F32),
            v((MODES, W), F32),
            v((3, 3, W), BF16),
            v((3, 3, W), BF16),
            v((W,), BF16),
            pltpu.SMEM((16,), jnp.int32),
            dma((31,)),
            dma((6,)), dma((6,)),
            dma((len(PIECES), 3)), dma((len(PIECES), 3)),
            dma((len(PIECES), 2)), dma((len(PIECES), 2)),
            dma((N - 1,)), dma((N - 1,)),
            dma((n_seq - 1,)), dma((n_seq - 1,)),
            dma((4,)),
        ],
        compiler_params=pltpu.CompilerParams(
            collective_id=0, has_side_effects=True, vmem_limit_bytes=60 * 1024 * 1024
        ),
        name="layers",
    )(
        residual_in, mr_query, mr_key, mr_value, mix_weight, li_weight, mr_filter, *tables, li_rate.T, li_residue.T,
        mr_short, li_short, norm_gain, decode_slot,
    )
    return pl.pallas_call(
        hand_over,
        out_shape=shapes,
        in_specs=[hbm] * 3,
        out_specs=(hbm,) * 3,
        scratch_shapes=[v((R, W), BF16), v((R, W), BF16), v((1, CB * MODES), F32), dma((2, 3))],
        compiler_params=pltpu.CompilerParams(vmem_limit_bytes=60 * 1024 * 1024),
        name="hand_over",
    )(*done)


def solution(mesh):
    in_specs = (
        P("seq", "chan"), P("seq", "chan"), P("seq", "chan"), P("seq", "chan"),
        P(None, None, "chan"), P(None, "chan"), P("chan", None), P("chan"),
        P(None, None, "chan"), P(None, None, "chan"), P("chan", None), P("chan", None), P("chan"),
    )
    out_specs = (P("seq", "chan"), P("seq", "chan"), P(("seq", "chan"), None))
    return jax.shard_map(
        functools.partial(local, mesh.shape["seq"]),
        mesh=mesh, in_specs=in_specs, out_specs=out_specs, check_vma=False,
    )
```
